128 devices in a mesh: grp: 2 (over z_lo), tok: 8 (over y, core), tp: 8 (over x, z_hi).
Axes of the slice: x: 4, y: 4, z: 4 (z_hi: 2, z_lo: 2; z = z_hi * 2 + z_lo), core: 2. Of those that a mesh axis runs over, the one named last changes fastest.
Arguments:
- teacher_in: bfloat16 [16384, 4096], P(('grp', 'tok'), 'tp'), may hold values from -11 to 11
- norm_gain: bfloat16 [4096], P('tp'), may hold values from 0.099609375 to 1.8984375
- w_qkv: bfloat16 [4096, 3, 2048], P(None, None, 'tp'), may hold values from -0.19018555 to 0.19018555
- probe: bfloat16 [2048, 1024], P('tp'), may hold values from -0.125 to 0.125
- student_in: bfloat16 [16384, 1024], P(('grp', 'tok', 'tp')), may hold values from -24 to 24
- w_up: bfloat16 [1024, 2048], replicated, may hold values from -0.1875 to 0.1875
- w_down: bfloat16 [2048, 1024], replicated, may hold values from -0.125 to 0.125
Outputs:
- loss: float32 [], replicated
- grad_up: float32 [1024, 2048], P(('grp', 'tok', 'tp'))
- grad_down: float32 [2048, 1024], P(('grp', 'tok', 'tp'))
The draws below stay inside these ranges and needn't reach their ends.
All inputs are finite; a program needn't handle non-finite values.
Results may differ from the reference program's by a relative error of at most 0.0044.
Values may be sent and summed in bfloat16 or wider, within the bound.
A program may use at most 192 MiB of HBM per device.

```python
import math
import jax
import jax.numpy as jnp
from jax import lax

D = 4096
HEADS = 16
HD = 128
DS = 1024
FF_S = 2048
HQ = 2048
SEQ = 8192
TOKENS = 16384
N_GRP = 2


def draw_teacher_in(key, part):
    key = jax.random.fold_in(key, 11)
    noise_key = jax.random.fold_in(key, 0)
    noise = jnp.clip(jax.random.normal(noise_key, (TOKENS, D), jnp.float32), -6.0, 6.0)
    return noise.astype(jnp.bfloat16)


def draw_w_qkv(key, part):
    key = jax.random.fold_in(key, 12)
    noise = jnp.clip(jax.random.normal(key, (D, 3, HQ), jnp.float32), -6.0, 6.0) * (4.0 / D) ** 0.5
    return noise.astype(jnp.bfloat16)


def strengthened(result, key, source, target, shards_of, factor):
    def block_of(dim):
        return (jnp.arange(result.shape[dim]) // (result.shape[dim] // shards_of)).reshape((-1,) + (1,) * (result.ndim - 1 - dim))

    near = jax.random.permutation(key, shards_of)[block_of(target)]
    far = (block_of(target) + shards_of // 2) % shards_of
    return jnp.where((block_of(source) == near) | (block_of(source) == far), factor * result, result)


def block_scale(own_key, dims, shards, least, high):
    level, own = 1.0, jax.random.fold_in(own_key, 6)
    for dim, parts in shards:
        steps = jnp.exp(jax.random.uniform(jax.random.fold_in(own, dim), (parts,), jnp.float32, least / len(shards), high / len(shards)))
        level = level * jnp.repeat(steps, dims[dim] // parts).reshape([-1 if axis == dim else 1 for axis in range(len(dims))])
    return level


def gaussian(stream_key, extent, spread, bound, shards=(), held_as=jnp.bfloat16):
    values = jax.random.normal(stream_key, extent, jnp.float32) * spread
    if len(shards) > 0:
        values = block_scale(stream_key, extent, shards, -0.22, 0.18) * values
    return jnp.clip(values, min=-bound, max=bound).astype(held_as)


def noise_with(rng, dims, scale, limit, cuts, heavy, held_as=jnp.bfloat16):
    values = scale * jax.random.normal(rng, dims, jnp.float32)
    if cuts:
        values = values * block_scale(rng, dims, cuts, -0.22, 0.18)
    return jnp.clip(strengthened(values, jax.random.fold_in(rng, 3), *heavy), -limit, limit).astype(held_as)


def setup_inputs(seed: int = 0) -> dict:
    key_of = jax.random.split(jax.random.key(seed), 8)
    return {
        "teacher_in": draw_teacher_in(jax.random.fold_in(key_of[7], 71), 0),
        "norm_gain": jnp.clip(1.0 + 0.18 * jax.random.normal(key_of[1], (D,), jnp.float32), 0.099609375, 1.8984375).astype(jnp.bfloat16),
        "w_qkv": draw_w_qkv(jax.random.fold_in(key_of[7], 71), 0),
        "probe": gaussian(key_of[3], (HQ, DS), HQ ** -0.5, 0.125, ((0, 8),)),
        "student_in": noise_with(key_of[4], (TOKENS, DS), 1.0, 24.0, ((0, 128),), (0, 1, 128, 5.5)),
        "w_up": gaussian(key_of[5], (DS, FF_S), DS ** -0.5, 0.1875),
        "w_down": gaussian(key_of[6], (FF_S, DS), FF_S ** -0.5, 0.125),
    }


def attend_block(query, keys, values):
    scores = jnp.dot(query.astype(jnp.float32), keys.astype(jnp.float32).T) * (1.0 / math.sqrt(HD))
    top = lax.optimization_barrier(jnp.max(scores, axis=-1, keepdims=True))
    expo = jnp.exp(scores - top)
    weights = (expo / lax.optimization_barrier(jnp.sum(expo, axis=-1, keepdims=True))).astype(jnp.bfloat16)
    return jnp.dot(weights, values, preferred_element_type=jnp.float32).astype(jnp.bfloat16)

def attend_head(triple):
    query, keys, values = triple
    block = min(512, SEQ)
    blocks = query.reshape(SEQ // block, block, HD)
    outs = lax.map(lambda piece: attend_block(piece, keys, values), blocks)
    return outs.reshape(SEQ, HD)

def reference(teacher_in, norm_gain, w_qkv, probe, student_in, w_up, w_down):
    x_full = teacher_in.astype(jnp.float32)
    scale = lax.rsqrt(lax.optimization_barrier(jnp.mean(x_full * x_full, axis=-1, keepdims=True)) + 1e-05)
    normed = (x_full * scale * norm_gain.astype(jnp.float32)).astype(jnp.bfloat16)
    qkv = jnp.dot(normed, w_qkv.reshape(D, 3 * HQ), preferred_element_type=jnp.float32).astype(jnp.bfloat16)
    qkv = qkv.reshape(N_GRP, SEQ, 3, HEADS, HD).transpose(2, 0, 3, 1, 4).reshape(3, N_GRP * HEADS, SEQ, HD)
    feats = lax.map(attend_head, (qkv[0], qkv[1], qkv[2]))
    features = feats.reshape(N_GRP, HEADS, SEQ, HD).transpose(0, 2, 1, 3).reshape(TOKENS, HQ)
    target = jnp.dot(features, probe, preferred_element_type=jnp.float32)
    hidden = jnp.dot(student_in, w_up, preferred_element_type=jnp.float32)
    act = jax.nn.gelu(hidden).astype(jnp.bfloat16)
    diff = jnp.dot(act, w_down, preferred_element_type=jnp.float32) - target
    loss = jnp.sum(diff * diff) / (TOKENS * DS)
    d_pred = (diff * (1.0 / math.sqrt(TOKENS))).astype(jnp.bfloat16)
    grad_down = jnp.dot(act.T, d_pred, preferred_element_type=jnp.float32)
    d_act = jnp.dot(d_pred, w_down.T, preferred_element_type=jnp.float32)
    d_hidden = jax.vjp(jax.nn.gelu, hidden)[1](d_act)[0].astype(jnp.bfloat16)
    grad_up = jnp.dot(student_in.T, d_hidden, preferred_element_type=jnp.float32)
    return (loss, grad_up, grad_down)
```

```python
import functools
import math

import jax
import jax.numpy as jnp
from jax import lax
from jax.experimental import pallas as pl
from jax.experimental.pallas import tpu as pltpu
from jax.sharding import PartitionSpec as P

HD = 128
EXP2_SCALE = math.log2(math.e) / math.sqrt(HD)


def attend_kernel(q_block, kv_block, q, kv, out):
    rows, width = q.shape
    blocks = kv.shape[0] // kv_block
    for head in range(width // HD):
        cols = slice(head * HD, (head + 1) * HD)
        vcols = slice(width + head * HD, width + (head + 1) * HD)

        def q_step(i, _):
            at = pl.ds(pl.multiple_of(i * q_block, q_block), q_block)
            query = q[at, cols]
            top = jnp.full((q_block, 1), -1e30, jnp.float32)
            total = jnp.zeros((q_block, HD), jnp.float32)
            acc = jnp.zeros((q_block, HD), jnp.float32)
            for j in range(blocks):
                keys = kv[j * kv_block : (j + 1) * kv_block, cols]
                values = kv[j * kv_block : (j + 1) * kv_block, vcols]
                scores = lax.dot_general(
                    query, keys, (((1,), (1,)), ((), ())), preferred_element_type=jnp.float32
                )
                top_new = jnp.maximum(top, jnp.max(scores, axis=1, keepdims=True))
                fade = jnp.exp2((top - top_new) * EXP2_SCALE)
                weights = jnp.exp2(scores * EXP2_SCALE - top_new * EXP2_SCALE).astype(jnp.bfloat16)
                both = jnp.concatenate([values, jnp.ones_like(values)], axis=1)
                res = jnp.dot(weights, both, preferred_element_type=jnp.float32)
                acc = acc * fade + res[:, :HD]
                total = total * fade + res[:, HD:]
                top = top_new
            out[at, cols] = (acc / total).astype(out.dtype)
            return 0

        lax.fori_loop(0, rows // q_block, q_step, 0)


def attend(query, keyvals):
    return pl.pallas_call(
        functools.partial(attend_kernel, 256, 1024),
        name="attend",
        out_shape=jax.ShapeDtypeStruct(query.shape, jnp.bfloat16),
        in_specs=[pl.BlockSpec(memory_space=pltpu.VMEM)] * 2,
        out_specs=pl.BlockSpec(memory_space=pltpu.VMEM),
        compiler_params=pltpu.CompilerParams(vmem_limit_bytes=48 << 20),
    )(query, keyvals)


def gelu_and_slope(hidden):
    act, pull = jax.vjp(jax.nn.gelu, hidden)
    return act, pull(jnp.ones_like(hidden))[0]


def on_device(teacher_in, norm_gain, w_qkv, probe, student_in, w_up, w_down):
    tps = lax.axis_size("tp")
    groups = lax.axis_size("grp") * lax.axis_size("tok")
    ff, ds = w_down.shape
    whole, gains = (
        lax.all_gather(teacher_in, "tp", axis=1, tiled=True),
        lax.all_gather(norm_gain, "tp", axis=0, tiled=True),
    )
    student = lax.all_gather(student_in, "tp", axis=0, tiled=True)
    x_full = whole.astype(jnp.float32)
    scale = lax.rsqrt(jnp.mean(x_full * x_full, axis=-1, keepdims=True) + 1e-05)
    normed = (x_full * scale * gains.astype(jnp.float32)).astype(jnp.bfloat16)
    width = w_qkv.shape[2]
    qkv = jnp.dot(
        normed, w_qkv.reshape(w_qkv.shape[0], 3 * width), preferred_element_type=jnp.float32
    ).astype(jnp.bfloat16)
    keyvals = lax.all_gather(qkv[:, width:], "tok", axis=0, tiled=True)
    features = attend(qkv[:, :width], keyvals)

    piece = ff // (groups * tps)
    me = lax.axis_index("tp")
    units = groups * piece
    unit = jnp.arange(units)
    unit = (unit // piece * tps + me) * piece + unit % piece
    pick = (jnp.arange(ff)[:, None] == unit[None, :]).astype(jnp.bfloat16)
    up = jnp.dot(w_up, pick, preferred_element_type=jnp.float32).astype(jnp.bfloat16)
    down = lax.dynamic_index_in_dim(
        w_down.reshape(groups, tps, piece, ds), me, axis=1, keepdims=False
    ).reshape(units, ds)
    tokens_all = student_in.shape[0] * groups * tps

    hidden = jnp.dot(student, up, preferred_element_type=jnp.float32)
    act, slope = gelu_and_slope(hidden)
    act = act.astype(jnp.bfloat16)
    part = jnp.dot(act, down, preferred_element_type=jnp.float32) - jnp.dot(
        features, probe, preferred_element_type=jnp.float32
    )
    diff = lax.psum_scatter(part, "tp", scatter_dimension=0, tiled=True)
    own_squares = jnp.sum(diff * diff)
    d_own = (diff * (1.0 / math.sqrt(tokens_all))).astype(jnp.bfloat16)
    d_pred = lax.all_gather(d_own, "tp", axis=0, tiled=True)
    grad_down = lax.psum_scatter(
        jnp.einsum("tr,tc->rc", act, d_pred, preferred_element_type=jnp.float32),
        ("grp", "tok"),
        scatter_dimension=0,
        tiled=True,
    )
    d_act = jnp.dot(d_pred, down.T, preferred_element_type=jnp.float32)
    d_hidden = (d_act * slope).astype(jnp.bfloat16)
    grad_up = lax.psum_scatter(
        jnp.einsum("tr,tc->rc", student, d_hidden, preferred_element_type=jnp.float32),
        ("grp", "tok"),
        scatter_dimension=0,
        tiled=True,
    )
    grad_up = lax.all_to_all(grad_up, "tp", split_axis=0, concat_axis=1, tiled=True)
    rows = grad_up.shape[0]
    grad_up = (
        grad_up.reshape(rows, tps, groups, piece).transpose(0, 2, 1, 3).reshape(rows, ff)
    )
    total_sq = lax.psum(own_squares, ("grp", "tok", "tp"))
    loss = total_sq / (tokens_all * ds)
    return (loss, grad_up, grad_down)


def solution(mesh):
    placed = (
        P(("grp", "tok"), "tp"),
        P("tp"),
        P(None, None, "tp"),
        P("tp", None),
        P(("grp", "tok", "tp"), None),
        P(),
        P(),
    )
    return jax.shard_map(
        on_device,
        mesh=mesh,
        in_specs=placed,
        out_specs=(P(), P(("grp", "tok", "tp"), None), P(("grp", "tok", "tp"), None)),
        check_vma=False,
    )
```

```python
import functools
import math

import jax
import jax.numpy as jnp
from jax import lax
from jax.experimental import pallas as pl
from jax.experimental.pallas import tpu as pltpu
from jax.sharding import PartitionSpec as P

HD = 128
EXP2_SCALE = math.log2(math.e) / math.sqrt(HD)


def attend_kernel(q_block, kv_block, q, kv, out):
    rows, width = q.shape
    blocks = kv.shape[0] // kv_block
    for head in range(width // HD):
        cols = slice(head * HD, (head + 1) * HD)
        vcols = slice(width + head * HD, width + (head + 1) * HD)

        def q_step(i, _):
            at = pl.ds(pl.multiple_of(i * q_block, q_block), q_block)
            query = q[at, cols]
            top = jnp.full((q_block, 1), -1e30, jnp.float32)
            total = jnp.zeros((q_block, HD), jnp.float32)
            acc = jnp.zeros((q_block, HD), jnp.float32)
            for j in range(blocks):
                keys = kv[j * kv_block : (j + 1) * kv_block, cols]
                values = kv[j * kv_block : (j + 1) * kv_block, vcols]
                scores = lax.dot_general(
                    query, keys, (((1,), (1,)), ((), ())), preferred_element_type=jnp.float32
                )
                top_new = jnp.maximum(top, jnp.max(scores, axis=1, keepdims=True))
                fade = jnp.exp2((top - top_new) * EXP2_SCALE)
                weights = jnp.exp2(scores * EXP2_SCALE - top_new * EXP2_SCALE).astype(jnp.bfloat16)
                both = jnp.concatenate([values, jnp.ones_like(values)], axis=1)
                res = jnp.dot(weights, both, preferred_element_type=jnp.float32)
                acc = acc * fade + res[:, :HD]
                total = total * fade + res[:, HD:]
                top = top_new
            out[at, cols] = (acc / total).astype(out.dtype)
            return 0

        lax.fori_loop(0, rows // q_block, q_step, 0)


def attend(query, keyvals):
    return pl.pallas_call(
        functools.partial(attend_kernel, 256, 1024),
        name="attend",
        out_shape=jax.ShapeDtypeStruct(query.shape, jnp.bfloat16),
        in_specs=[pl.BlockSpec(memory_space=pltpu.VMEM)] * 2,
        out_specs=pl.BlockSpec(memory_space=pltpu.VMEM),
        compiler_params=pltpu.CompilerParams(vmem_limit_bytes=48 << 20),
    )(query, keyvals)

MESH = pl.DeviceIdType.MESH


def tail_kernel(
    sizes, student, act, slope, feats, down, probe, loss, up_out, down_out,
    outgo, income, d_all, acc_down, acc_up, core_down, core_up,
    mine_down, mine_up, sent_down, sent_up, got_down, got_up, up_rows, up_got,
    loss_tp, loss_core, loss_gy,
    rs_s, rs_r, ag_s, ag_r, lt_s, lt_r, co_s, co_r, gy_s, gy_r, aa_s, aa_r,
):
    grps, toks, tps = sizes
    ys = toks // 2
    gys = grps * ys
    grp, tok, tp = lax.axis_index("grp"), lax.axis_index("tok"), lax.axis_index("tp")
    core, gy = lax.rem(tok, 2), grp * ys + tok // 2
    block = outgo.shape[1]

    def tp_peer(d):
        return lax.rem(tp + d, tps)

    def gy_peer(d):
        return lax.rem(gy + d, gys)

    def at_gy(to):
        return (to // ys, lax.rem(to, ys) * 2 + core, tp)

    sibling = (grp, tok + 1 - 2 * core, tp)

    barrier = pltpu.get_barrier_semaphore()
    for d in range(1, tps):
        pl.semaphore_signal(barrier, inc=1, device_id=(grp, tok, tp_peer(d)), device_id_type=MESH)
    for d in range(1, gys):
        pl.semaphore_signal(barrier, inc=1, device_id=at_gy(gy_peer(d)), device_id_type=MESH)
    pl.semaphore_signal(barrier, inc=1, device_id=sibling, device_id_type=MESH)

    def send(src, dst, ssem, rsem, device):
        copy = pltpu.make_async_remote_copy(
            src_ref=src, dst_ref=dst, send_sem=ssem, recv_sem=rsem,
            device_id=device, device_id_type=MESH,
        )
        copy.start()
        return copy

    def part_of(q):
        rows = pl.ds(pl.multiple_of(q * block, block), block)
        return jnp.dot(act[rows, :], down[...], preferred_element_type=jnp.float32) - jnp.dot(
            feats[rows, :], probe[...], preferred_element_type=jnp.float32
        )

    copies = []
    for d in range(1, tps):
        q = tp_peer(d)
        outgo[d] = part_of(q).astype(outgo.dtype)
        if d == 1:
            pl.semaphore_wait(barrier, tps + gys - 1)
        copies.append(
            send(outgo.at[d], income.at[d], rs_s.at[d], rs_r.at[d], (grp, tok, q))
        )
    diff = part_of(tp)
    for copy in copies:
        copy.wait_recv()
    for d in range(1, tps):
        diff = diff + income[d].astype(jnp.float32)
    squares = jnp.sum((diff * diff).reshape(block // 8, 8, diff.shape[1]), axis=0)
    loss_tp[tp] = sum(squares[:, i * 128 : (i + 1) * 128] for i in range(diff.shape[1] // 128))
    d_all[tp] = (diff * (1.0 / math.sqrt(block * tps * toks * grps))).astype(d_all.dtype)
    gathers = []
    for d in range(1, tps):
        to = (grp, tok, tp_peer(d))
        gathers.append(send(d_all.at[tp], d_all.at[tp], ag_s.at[d], ag_r.at[d], to))
        gathers.append(send(loss_tp.at[tp], loss_tp.at[tp], lt_s.at[d], lt_r.at[d], to))
    for copy in gathers:
        copy.wait_recv()

    d_pred = d_all[...].reshape(act.shape[0], down.shape[1])
    acc_down[...] = lax.dot_general(
        act[...], d_pred, (((0,), (0,)), ((), ())), preferred_element_type=jnp.float32
    ).reshape(acc_down.shape)
    loss_core[core] = sum(loss_tp[i] for i in range(tps))
    pair = [
        send(acc_down.at[:, 1 - core], core_down, co_s.at[0], co_r.at[0], sibling),
        send(loss_core.at[core], loss_core.at[core], co_s.at[1], co_r.at[1], sibling),
    ]
    d_act = lax.dot_general(
        d_pred, down[...], (((1,), (1,)), ((), ())), preferred_element_type=jnp.float32
    )
    d_hidden = (d_act * slope[...]).astype(jnp.bfloat16)
    acc_up[...] = lax.dot_general(
        student[...], d_hidden, (((0,), (0,)), ((), ())), preferred_element_type=jnp.float32
    ).reshape(acc_up.shape)
    pair.append(send(acc_up.at[:, 1 - core], core_up, co_s.at[2], co_r.at[2], sibling))

    pair[0].wait_recv()
    pair[1].wait_recv()
    mine_down[...] = acc_down[:, core] + core_down[...]
    sent_down[...] = mine_down[...].astype(sent_down.dtype)
    loss_gy[gy] = loss_core[0] + loss_core[1]
    far = []
    for d in range(1, gys):
        to = gy_peer(d)
        far.append(send(sent_down.at[to], got_down.at[d], gy_s.at[0, d], gy_r.at[0, d], at_gy(to)))
        far.append(send(loss_gy.at[gy], loss_gy.at[gy], gy_s.at[1, d], gy_r.at[1, d], at_gy(to)))
    pair[2].wait_recv()
    mine_up[...] = acc_up[:, core] + core_up[...]
    sent_up[...] = mine_up[...].astype(sent_up.dtype)
    far_up = []
    for d in range(1, gys):
        to = gy_peer(d)
        far_up.append(send(sent_up.at[to], got_up.at[d], gy_s.at[2, d], gy_r.at[2, d], at_gy(to)))
    for copy in far_up:
        copy.wait_recv()
    total = mine_up[gy]
    for d in range(1, gys):
        total = total + got_up[d].astype(jnp.float32)
    up_rows[...] = total.reshape(up_rows.shape)
    last = []
    for d in range(1, tps):
        q = tp_peer(d)
        last.append(send(up_rows.at[q], up_got.at[tp], aa_s.at[d], aa_r.at[d], (grp, tok, q)))
    for copy in far:
        copy.wait_recv()
    total = mine_down[gy]
    for d in range(1, gys):
        total = total + got_down[d].astype(jnp.float32)
    down_out[...] = total
    loss[...] = sum(loss_gy[i] for i in range(gys))
    up_got[tp] = up_rows[tp]
    for copy in last:
        copy.wait_recv()
    up_out[...] = up_got[...]
    for copy in copies + gathers + pair + far + far_up + last:
        copy.wait_send()


def tail(sizes, student, act, slope, feats, down, probe):
    grps, toks, tps = sizes
    gys = grps * toks // 2
    rows, ds = student.shape
    units = act.shape[1]
    block, piece, strip = rows // tps, units // (gys * 2), ds // (gys * 2)
    f32, bf16 = jnp.float32, jnp.bfloat16
    dma = pltpu.SemaphoreType.DMA
    return pl.pallas_call(
        functools.partial(tail_kernel, sizes),
        name="student_tail",
        out_shape=(
            jax.ShapeDtypeStruct((8, 128), f32),
            jax.ShapeDtypeStruct((tps, strip // tps, units), f32),
            jax.ShapeDtypeStruct((piece, ds), f32),
        ),
        in_specs=[pl.BlockSpec(memory_space=pltpu.VMEM)] * 6,
        out_specs=[pl.BlockSpec(memory_space=pltpu.VMEM)] * 3,
        scratch_shapes=[
            pltpu.VMEM((tps, block, ds), bf16),
            pltpu.VMEM((tps, block, ds), bf16),
            pltpu.VMEM((tps, block, ds), bf16),
            pltpu.VMEM((gys, 2, piece, ds), f32),
            pltpu.VMEM((gys, 2, strip, units), f32),
            pltpu.VMEM((gys, piece, ds), f32),
            pltpu.VMEM((gys, strip, units), f32),
            pltpu.VMEM((gys, piece, ds), f32),
            pltpu.VMEM((gys, strip, units), f32),
            pltpu.VMEM((gys, piece, ds), bf16),
            pltpu.VMEM((gys, strip, units), bf16),
            pltpu.VMEM((gys, piece, ds), bf16),
            pltpu.VMEM((gys, strip, units), bf16),
            pltpu.VMEM((tps, strip // tps, units), f32),
            pltpu.VMEM((tps, strip // tps, units), f32),
            pltpu.VMEM((tps, 8, 128), f32),
            pltpu.VMEM((2, 8, 128), f32),
            pltpu.VMEM((gys, 8, 128), f32),
            dma((tps,)), dma((tps,)), dma((tps,)), dma((tps,)), dma((tps,)), dma((tps,)),
            dma((3,)), dma((3,)), dma((3, gys)), dma((3, gys)), dma((tps,)), dma((tps,)),
        ],
        compiler_params=pltpu.CompilerParams(
            collective_id=1, has_side_effects=True, vmem_limit_bytes=48 << 20
        ),
    )(student, act, slope, feats, down, probe)


def gelu_and_slope(hidden):
    act, pull = jax.vjp(jax.nn.gelu, hidden)
    return act, pull(jnp.ones_like(hidden))[0]


def on_device(teacher_in, norm_gain, w_qkv, probe, student_in, w_up, w_down):
    tps = lax.axis_size("tp")
    groups = lax.axis_size("grp") * lax.axis_size("tok")
    ff, ds = w_down.shape
    whole, gains = (
        lax.all_gather(teacher_in, "tp", axis=1, tiled=True),
        lax.all_gather(norm_gain, "tp", axis=0, tiled=True),
    )
    student = lax.all_gather(student_in, "tp", axis=0, tiled=True)
    x_full = whole.astype(jnp.float32)
    scale = lax.rsqrt(jnp.mean(x_full * x_full, axis=-1, keepdims=True) + 1e-05)
    normed = (x_full * scale * gains.astype(jnp.float32)).astype(jnp.bfloat16)
    width = w_qkv.shape[2]
    qkv = jnp.dot(
        normed, w_qkv.reshape(w_qkv.shape[0], 3 * width), preferred_element_type=jnp.float32
    ).astype(jnp.bfloat16)
    keyvals = lax.all_gather(qkv[:, width:], "tok", axis=0, tiled=True)
    features = attend(qkv[:, :width], keyvals)

    piece = ff // (groups * tps)
    me = lax.axis_index("tp")
    units = groups * piece
    unit = jnp.arange(units)
    unit = (unit // piece * tps + me) * piece + unit % piece
    pick = (jnp.arange(ff)[:, None] == unit[None, :]).astype(jnp.bfloat16)
    up = jnp.dot(w_up, pick, preferred_element_type=jnp.float32).astype(jnp.bfloat16)
    down = lax.dynamic_index_in_dim(
        w_down.reshape(groups, tps, piece, ds), me, axis=1, keepdims=False
    ).reshape(units, ds)
    tokens_all = student_in.shape[0] * groups * tps

    hidden = jnp.dot(student, up, preferred_element_type=jnp.float32)
    act, slope = gelu_and_slope(hidden)
    act = act.astype(jnp.bfloat16)
    sizes = (lax.axis_size("grp"), lax.axis_size("tok"), tps)
    squares, grad_up, grad_down = tail(sizes, student, act, slope, features, down, probe)
    grad_up = (
        grad_up.reshape(tps, -1, groups, piece).transpose(1, 2, 0, 3).reshape(-1, ff)
    )
    loss = jnp.sum(squares) / (tokens_all * ds)
    return (loss, grad_up, grad_down)


def solution(mesh):
    placed = (
        P(("grp", "tok"), "tp"),
        P("tp"),
        P(None, None, "tp"),
        P("tp", None),
        P(("grp", "tok", "tp"), None),
        P(),
        P(),
    )
    return jax.shard_map(
        on_device,
        mesh=mesh,
        in_specs=placed,
        out_specs=(P(), P(("grp", "tok", "tp"), None), P(("grp", "tok", "tp"), None)),
        check_vma=False,
    )
```

```python
import functools
import math

import jax
import jax.numpy as jnp
from jax import lax
from jax.experimental import pallas as pl
from jax.experimental.pallas import tpu as pltpu
from jax.sharding import PartitionSpec as P

HD = 128
EXP2_SCALE = math.log2(math.e) / math.sqrt(HD)


MESH = pl.DeviceIdType.MESH


def teacher_kernel(
    sizes, firsts, plan, teacher_in, gain, w_hbm, feats,
    xb, gains, w, normed, qb, kvb, top_s, sum_s, acc_s,
    xs, xr, gs, gr, ks, kr, local,
):
    grps, toks, tps = sizes
    grp, tok, tp = lax.axis_index("grp"), lax.axis_index("tok"), lax.axis_index("tp")
    chunk, feat = xb.shape[2], xb.shape[3]
    half = chunk // 2
    width = qb.shape[2]
    heads = width // HD
    zh, x = lax.rem(tp, 2), tp // 2
    core, y = lax.rem(tok, 2), tok // 2
    zp = tp + 1 - 2 * zh

    def along_x(d):
        return lax.rem(x + d, tps // 2) * 2 + zh

    def along_y(d):
        return lax.rem(y + d, toks // 2) * 2 + core

    def other(slot):
        return slot + 1 - 2 * zh

    right, left, across = along_x(1), along_x(3), along_x(2)
    up, down, yfar = along_y(1), along_y(3), along_y(2)
    to_z, to_right, to_left = (grp, tok, zp), (grp, tok, right), (grp, tok, left)
    to_up, to_down, to_sib = (grp, up, tp), (grp, down, tp), (grp, tok + 1 - 2 * core, tp)

    fetch = pltpu.make_async_copy(w_hbm, w, local.at[0])
    fetch.start()
    keep = [
        pltpu.make_async_copy(
            teacher_in.at[pl.ds(c * chunk, chunk), :], xb.at[c, tp], local.at[1 + c]
        )
        for c in range(len(firsts))
    ]
    for copy in keep:
        copy.start()
    gains[tp] = gain[...]

    barrier = pltpu.get_barrier_semaphore()
    greet = [(grp, tok, lax.rem(tp + d, tps)) for d in range(1, tps)] + [to_up, to_down, to_sib]
    for device in greet:
        pl.semaphore_signal(barrier, inc=1, device_id=device, device_id_type=MESH)
    pl.semaphore_wait(barrier, len(greet))

    sent = {}

    def send(name, src, dst, ssem, rsem, device):
        copy = pltpu.make_async_remote_copy(
            src_ref=src, dst_ref=dst, send_sem=ssem, recv_sem=rsem,
            device_id=device, device_id_type=MESH,
        )
        copy.start()
        sent[name] = copy

    def arrived(*names):
        for name in names:
            sent[name].wait_recv()

    names_x = ("z0", "z1", "z2", "z3", "r0", "l0", "r1", "l1", "fr0", "fr1", "fl0", "fl1")
    names_k = ("s0", "s1", "s2", "s3", "u0", "d0", "fu", "fd")

    def send_x(name, c, ref, device):
        i = names_x.index(name)
        send((name, c), ref[0], ref[1], xs.at[c, i], xr.at[c, i], device)

    def send_k(name, c, ref, device):
        i = names_k.index(name)
        send((name, c), ref, ref, ks.at[c, i], kr.at[c, i], device)

    def own(c):
        return teacher_in.at[pl.ds(c * chunk, chunk), :], xb.at[c, tp]

    def slot(c, p):
        return xb.at[c, p], xb.at[c, p]

    def part(c, p, h):
        ref = xb.at[c, p, pl.ds(h * half, half), :]
        return ref, ref

    def x0(c):
        if firsts[c] == "z":
            send_x("z0", c, own(c), to_z)
        send_x("r0", c, own(c), to_right)
        send_x("l0", c, own(c), to_left)
        if firsts[c] == "x":
            send_x("z0", c, own(c), to_z)

    def x1(c):
        if firsts[c] == "z":
            arrived(("z0", c))
            send_x("r1", c, slot(c, zp), to_right)
            send_x("l1", c, slot(c, zp), to_left)
        else:
            arrived(("r0", c))
            send_x("fr0", c, part(c, left, 0), to_right)
            send_x("z1", c, slot(c, left), to_z)
            arrived(("l0", c))
            send_x("fl0", c, part(c, right, 1), to_left)
            send_x("z2", c, slot(c, right), to_z)

    def x2(c):
        if firsts[c] == "z":
            arrived(("r0", c))
            send_x("fr0", c, part(c, left, 0), to_right)
            arrived(("l0", c))
            send_x("fl0", c, part(c, right, 1), to_left)
            arrived(("r1", c))
            send_x("fr1", c, part(c, other(left), 0), to_right)
            arrived(("l1", c))
            send_x("fl1", c, part(c, other(right), 1), to_left)
        else:
            arrived(("fr0", c), ("fl0", c))
            send_x("z3", c, slot(c, across), to_z)

    def x3(c):
        if firsts[c] == "z":
            arrived(("fr0", c), ("fl0", c), ("fr1", c), ("fl1", c))
        else:
            arrived(("z0", c), ("z1", c), ("z2", c), ("z3", c))

    def project(c):
        keep[c].wait()
        if c == 0:
            for d in range(1, tps):
                arrived(("g", d))
            fetch.wait()
        step = 64

        def rows_of(i, _):
            rows = pl.ds(pl.multiple_of(i * step, step), step)
            squares = jnp.zeros((step, feat), jnp.float32)
            for p in range(tps):
                part_x = xb[c, p, rows, :].astype(jnp.float32)
                squares = squares + part_x * part_x
            mean = jnp.sum(squares, axis=1, keepdims=True) / (tps * feat)
            scale = lax.rsqrt(mean + 1e-05)
            for p in range(tps):
                part_x = xb[c, p, rows, :].astype(jnp.float32)
                normed[rows, p * feat : (p + 1) * feat] = (
                    part_x * scale * gains[p, 0:1, :]
                ).astype(jnp.bfloat16)
            return 0

        lax.fori_loop(0, chunk // step, rows_of, 0)
        kvb[c, tok] = jnp.dot(
            normed[...], w[:, width:], preferred_element_type=jnp.float32
        ).astype(jnp.bfloat16)
        send_k("u0", c, kvb.at[c, tok], to_up)
        send_k("d0", c, kvb.at[c, tok], to_down)
        send_k("s0", c, kvb.at[c, tok], to_sib)
        qb[c] = jnp.dot(
            normed[...], w[:, :width], preferred_element_type=jnp.float32
        ).astype(jnp.bfloat16)

    def k1(c):
        arrived(("u0", c))
        send_k("fu", c, kvb.at[c, down, pl.ds(0, half), :], to_up)
        send_k("s1", c, kvb.at[c, down], to_sib)
        arrived(("d0", c))
        send_k("fd", c, kvb.at[c, up, pl.ds(half, half), :], to_down)
        send_k("s2", c, kvb.at[c, up], to_sib)

    def k2(c):
        arrived(("fu", c), ("fd", c))
        send_k("s3", c, kvb.at[c, yfar], to_sib)

    def k3(c):
        arrived(("s0", c), ("s1", c), ("s2", c), ("s3", c))

    def attend(i, c):
        for head in range(heads):
            cols = slice(head * HD, (head + 1) * HD)
            vcols = slice(width + head * HD, width + (head + 1) * HD)
            query = qb[i, :, cols]
            top, total, acc = top_s[i, head][:, :1], sum_s[i, head], acc_s[i, head]
            for j in range(2):
                slots = slice(j * toks // 2, (j + 1) * toks // 2)
                keys = kvb[c, slots, :, cols].reshape(toks // 2 * chunk, HD)
                values = kvb[c, slots, :, vcols].reshape(toks // 2 * chunk, HD)
                scores = lax.dot_general(
                    query, keys, (((1,), (1,)), ((), ())), preferred_element_type=jnp.float32
                )
                top_new = jnp.maximum(top, jnp.max(scores, axis=1, keepdims=True))
                fade = jnp.exp2((top - top_new) * EXP2_SCALE)
                weights = jnp.exp2(scores * EXP2_SCALE - top_new * EXP2_SCALE).astype(jnp.bfloat16)
                both = jnp.concatenate([values, jnp.ones_like(values)], axis=1)
                res = jnp.dot(weights, both, preferred_element_type=jnp.float32)
                acc = acc * fade + res[:, :HD]
                total = total * fade + res[:, HD:]
                top = top_new
            top_s[i, head] = jnp.broadcast_to(top, (chunk, HD))
            sum_s[i, head] = total
            acc_s[i, head] = acc

    def queries(lo, hi, c):
        lax.fori_loop(lo, hi, lambda i, _: (attend(i, c), 0)[1], 0)

    def keys(i, lo, hi):
        lax.fori_loop(lo, hi, lambda c, _: (attend(i, c), 0)[1], 0)

    def greetings():
        for d in range(1, tps):
            i = lax.rem(tp + d, tps)
            send(("g", d), gains.at[tp], gains.at[tp], gs.at[d], gr.at[d], (grp, tok, i))
        top_s[...] = jnp.full(top_s.shape, -1e30, jnp.float32)
        sum_s[...] = jnp.zeros(sum_s.shape, jnp.float32)
        acc_s[...] = jnp.zeros(acc_s.shape, jnp.float32)

    steps = dict(
        x0=x0, x1=x1, x2=x2, x3=x3, p=project, k1=k1, k2=k2, k3=k3,
        qs=queries, ks=keys, g=greetings,
    )
    for step in plan:
        steps[step[0]](*step[1:])
    for i in range(len(firsts)):
        for head in range(heads):
            feats[i * chunk : (i + 1) * chunk, head * HD : (head + 1) * HD] = (
                acc_s[i, head] / sum_s[i, head]
            ).astype(feats.dtype)
    for copy in sent.values():
        copy.wait_send()


FIRSTS = ("z", "x", "z", "x")
PLAN = (
    ("x0", 0), ("g",), ("x0", 1),
    ("x1", 0), ("x2", 0), ("x0", 2), ("x1", 1), ("x3", 0), ("p", 0),
    ("x2", 1), ("x0", 3), ("x1", 2), ("k1", 0), ("x3", 1), ("p", 1), ("k2", 0),
    ("x2", 2), ("x1", 3), ("k1", 1), ("k3", 0), ("qs", 0, 1, 0), ("k2", 1),
    ("x3", 2), ("p", 2),
    ("x2", 3), ("qs", 1, 2, 0), ("k1", 2), ("k3", 1), ("qs", 0, 2, 1), ("k2", 2),
    ("x3", 3), ("p", 3), ("k3", 2),
    ("ks", 2, 0, 3), ("k1", 3), ("qs", 0, 2, 2), ("k2", 3), ("ks", 3, 0, 3),
    ("k3", 3), ("qs", 0, 4, 3),
)


def teacher(sizes, teacher_in, gain, w):
    grps, toks, tps = sizes
    rows, feat = teacher_in.shape
    depth, width = w.shape[0], w.shape[1] // 3
    chunks, heads = len(FIRSTS), width // HD
    chunk = rows // chunks
    f32, bf16 = jnp.float32, jnp.bfloat16
    dma = pltpu.SemaphoreType.DMA
    vmem = pl.BlockSpec(memory_space=pltpu.VMEM)
    return pl.pallas_call(
        functools.partial(teacher_kernel, sizes, FIRSTS, PLAN),
        name="teacher",
        out_shape=jax.ShapeDtypeStruct((rows, width), bf16),
        in_specs=[vmem, vmem, pl.BlockSpec(memory_space=pl.ANY)],
        out_specs=vmem,
        scratch_shapes=[
            pltpu.VMEM((chunks, tps, chunk, feat), bf16),
            pltpu.VMEM((tps, 8, feat), f32),
            pltpu.VMEM((depth, 3 * width), bf16),
            pltpu.VMEM((chunk, depth), bf16),
            pltpu.VMEM((chunks, chunk, width), bf16),
            pltpu.VMEM((chunks, toks, chunk, 2 * width), bf16),
            pltpu.VMEM((chunks, heads, chunk, HD), f32),
            pltpu.VMEM((chunks, heads, chunk, HD), f32),
            pltpu.VMEM((chunks, heads, chunk, HD), f32),
            dma((chunks, 12)), dma((chunks, 12)), dma((tps,)), dma((tps,)),
            dma((chunks, 8)), dma((chunks, 8)), dma((1 + chunks,)),
        ],
        compiler_params=pltpu.CompilerParams(
            collective_id=2, has_side_effects=True, vmem_limit_bytes=56 << 20
        ),
    )(teacher_in, gain, w)


def tail_kernel(
    sizes, student, act, slope, feats, down, probe, loss, up_out, down_out,
    outgo, income, d_all, acc_down, acc_up, core_down, core_up,
    mine_down, mine_up, sent_down, sent_up, got_down, got_up, up_rows, up_got,
    loss_tp, loss_core, loss_gy,
    rs_s, rs_r, ag_s, ag_r, lt_s, lt_r, co_s, co_r, gy_s, gy_r, aa_s, aa_r,
):
    grps, toks, tps = sizes
    ys = toks // 2
    gys = grps * ys
    grp, tok, tp = lax.axis_index("grp"), lax.axis_index("tok"), lax.axis_index("tp")
    core, gy = lax.rem(tok, 2), grp * ys + tok // 2
    block = outgo.shape[1]

    def tp_peer(d):
        return lax.rem(tp + d, tps)

    def gy_peer(d):
        return lax.rem(gy + d, gys)

    def at_gy(to):
        return (to // ys, lax.rem(to, ys) * 2 + core, tp)

    sibling = (grp, tok + 1 - 2 * core, tp)

    barrier = pltpu.get_barrier_semaphore()
    for d in range(1, tps):
        pl.semaphore_signal(barrier, inc=1, device_id=(grp, tok, tp_peer(d)), device_id_type=MESH)
    for d in range(1, gys):
        pl.semaphore_signal(barrier, inc=1, device_id=at_gy(gy_peer(d)), device_id_type=MESH)
    pl.semaphore_signal(barrier, inc=1, device_id=sibling, device_id_type=MESH)

    def send(src, dst, ssem, rsem, device):
        copy = pltpu.make_async_remote_copy(
            src_ref=src, dst_ref=dst, send_sem=ssem, recv_sem=rsem,
            device_id=device, device_id_type=MESH,
        )
        copy.start()
        return copy

    def part_of(q):
        rows = pl.ds(pl.multiple_of(q * block, block), block)
        return jnp.dot(act[rows, :], down[...], preferred_element_type=jnp.float32) - jnp.dot(
            feats[rows, :], probe[...], preferred_element_type=jnp.float32
        )

    copies = []
    for d in range(1, tps):
        q = tp_peer(d)
        outgo[d] = part_of(q).astype(outgo.dtype)
        if d == 1:
            pl.semaphore_wait(barrier, tps + gys - 1)
        copies.append(
            send(outgo.at[d], income.at[d], rs_s.at[d], rs_r.at[d], (grp, tok, q))
        )
    diff = part_of(tp)
    for copy in copies:
        copy.wait_recv()
    for d in range(1, tps):
        diff = diff + income[d].astype(jnp.float32)
    squares = jnp.sum((diff * diff).reshape(block // 8, 8, diff.shape[1]), axis=0)
    loss_tp[tp] = sum(squares[:, i * 128 : (i + 1) * 128] for i in range(diff.shape[1] // 128))
    d_all[tp] = (diff * (1.0 / math.sqrt(block * tps * toks * grps))).astype(d_all.dtype)
    gathers = []
    for d in range(1, tps):
        to = (grp, tok, tp_peer(d))
        gathers.append(send(d_all.at[tp], d_all.at[tp], ag_s.at[d], ag_r.at[d], to))
        gathers.append(send(loss_tp.at[tp], loss_tp.at[tp], lt_s.at[d], lt_r.at[d], to))
    for copy in gathers:
        copy.wait_recv()

    d_pred = d_all[...].reshape(act.shape[0], down.shape[1])
    acc_down[...] = lax.dot_general(
        act[...], d_pred, (((0,), (0,)), ((), ())), preferred_element_type=jnp.float32
    ).reshape(acc_down.shape)
    loss_core[core] = sum(loss_tp[i] for i in range(tps))
    pair = [
        send(acc_down.at[:, 1 - core], core_down, co_s.at[0], co_r.at[0], sibling),
        send(loss_core.at[core], loss_core.at[core], co_s.at[1], co_r.at[1], sibling),
    ]
    d_act = lax.dot_general(
        d_pred, down[...], (((1,), (1,)), ((), ())), preferred_element_type=jnp.float32
    )
    d_hidden = (d_act * slope[...]).astype(jnp.bfloat16)
    acc_up[...] = lax.dot_general(
        student[...], d_hidden, (((0,), (0,)), ((), ())), preferred_element_type=jnp.float32
    ).reshape(acc_up.shape)
    pair.append(send(acc_up.at[:, 1 - core], core_up, co_s.at[2], co_r.at[2], sibling))

    pair[0].wait_recv()
    pair[1].wait_recv()
    mine_down[...] = acc_down[:, core] + core_down[...]
    sent_down[...] = mine_down[...].astype(sent_down.dtype)
    loss_gy[gy] = loss_core[0] + loss_core[1]
    far = []
    for d in range(1, gys):
        to = gy_peer(d)
        far.append(send(sent_down.at[to], got_down.at[d], gy_s.at[0, d], gy_r.at[0, d], at_gy(to)))
        far.append(send(loss_gy.at[gy], loss_gy.at[gy], gy_s.at[1, d], gy_r.at[1, d], at_gy(to)))
    pair[2].wait_recv()
    mine_up[...] = acc_up[:, core] + core_up[...]
    sent_up[...] = mine_up[...].astype(sent_up.dtype)
    far_up = []
    for d in range(1, gys):
        to = gy_peer(d)
        far_up.append(send(sent_up.at[to], got_up.at[d], gy_s.at[2, d], gy_r.at[2, d], at_gy(to)))
    for copy in far_up:
        copy.wait_recv()
    total = mine_up[gy]
    for d in range(1, gys):
        total = total + got_up[d].astype(jnp.float32)
    up_rows[...] = total.reshape(up_rows.shape)
    last = []
    for d in range(1, tps):
        q = tp_peer(d)
        last.append(send(up_rows.at[q], up_got.at[tp], aa_s.at[d], aa_r.at[d], (grp, tok, q)))
    for copy in far:
        copy.wait_recv()
    total = mine_down[gy]
    for d in range(1, gys):
        total = total + got_down[d].astype(jnp.float32)
    down_out[...] = total
    loss[...] = sum(loss_gy[i] for i in range(gys))
    up_got[tp] = up_rows[tp]
    for copy in last:
        copy.wait_recv()
    up_out[...] = up_got[...]
    for copy in copies + gathers + pair + far + far_up + last:
        copy.wait_send()


def tail(sizes, student, act, slope, feats, down, probe):
    grps, toks, tps = sizes
    gys = grps * toks // 2
    rows, ds = student.shape
    units = act.shape[1]
    block, piece, strip = rows // tps, units // (gys * 2), ds // (gys * 2)
    f32, bf16 = jnp.float32, jnp.bfloat16
    dma = pltpu.SemaphoreType.DMA
    return pl.pallas_call(
        functools.partial(tail_kernel, sizes),
        name="student_tail",
        out_shape=(
            jax.ShapeDtypeStruct((8, 128), f32),
            jax.ShapeDtypeStruct((tps, strip // tps, units), f32),
            jax.ShapeDtypeStruct((piece, ds), f32),
        ),
        in_specs=[pl.BlockSpec(memory_space=pltpu.VMEM)] * 6,
        out_specs=[pl.BlockSpec(memory_space=pltpu.VMEM)] * 3,
        scratch_shapes=[
            pltpu.VMEM((tps, block, ds), bf16),
            pltpu.VMEM((tps, block, ds), bf16),
            pltpu.VMEM((tps, block, ds), bf16),
            pltpu.VMEM((gys, 2, piece, ds), f32),
            pltpu.VMEM((gys, 2, strip, units), f32),
            pltpu.VMEM((gys, piece, ds), f32),
            pltpu.VMEM((gys, strip, units), f32),
            pltpu.VMEM((gys, piece, ds), f32),
            pltpu.VMEM((gys, strip, units), f32),
            pltpu.VMEM((gys, piece, ds), bf16),
            pltpu.VMEM((gys, strip, units), bf16),
            pltpu.VMEM((gys, piece, ds), bf16),
            pltpu.VMEM((gys, strip, units), bf16),
            pltpu.VMEM((tps, strip // tps, units), f32),
            pltpu.VMEM((tps, strip // tps, units), f32),
            pltpu.VMEM((tps, 8, 128), f32),
            pltpu.VMEM((2, 8, 128), f32),
            pltpu.VMEM((gys, 8, 128), f32),
            dma((tps,)), dma((tps,)), dma((tps,)), dma((tps,)), dma((tps,)), dma((tps,)),
            dma((3,)), dma((3,)), dma((3, gys)), dma((3, gys)), dma((tps,)), dma((tps,)),
        ],
        compiler_params=pltpu.CompilerParams(
            collective_id=1, has_side_effects=True, vmem_limit_bytes=48 << 20
        ),
    )(student, act, slope, feats, down, probe)


def gelu_and_slope(hidden):
    act, pull = jax.vjp(jax.nn.gelu, hidden)
    return act, pull(jnp.ones_like(hidden))[0]


def on_device(teacher_in, norm_gain, w_qkv, probe, student_in, w_up, w_down):
    tps = lax.axis_size("tp")
    groups = lax.axis_size("grp") * lax.axis_size("tok")
    ff, ds = w_down.shape
    sizes = (lax.axis_size("grp"), lax.axis_size("tok"), tps)
    student = lax.all_gather(student_in, "tp", axis=0, tiled=True)
    gain = jnp.broadcast_to(norm_gain.astype(jnp.float32)[None, :], (8, norm_gain.shape[0]))
    features = teacher(sizes, teacher_in, gain, w_qkv.reshape(w_qkv.shape[0], -1))

    piece = ff // (groups * tps)
    me = lax.axis_index("tp")
    units = groups * piece
    unit = jnp.arange(units)
    unit = (unit // piece * tps + me) * piece + unit % piece
    pick = (jnp.arange(ff)[:, None] == unit[None, :]).astype(jnp.bfloat16)
    up = jnp.dot(w_up, pick, preferred_element_type=jnp.float32).astype(jnp.bfloat16)
    down = lax.dynamic_index_in_dim(
        w_down.reshape(groups, tps, piece, ds), me, axis=1, keepdims=False
    ).reshape(units, ds)
    tokens_all = student_in.shape[0] * groups * tps

    hidden = jnp.dot(student, up, preferred_element_type=jnp.float32)
    act, slope = gelu_and_slope(hidden)
    act = act.astype(jnp.bfloat16)
    squares, grad_up, grad_down = tail(sizes, student, act, slope, features, down, probe)
    grad_up = (
        grad_up.reshape(tps, -1, groups, piece).transpose(1, 2, 0, 3).reshape(-1, ff)
    )
    loss = jnp.sum(squares) / (tokens_all * ds)
    return (loss, grad_up, grad_down)


def solution(mesh):
    placed = (
        P(("grp", "tok"), "tp"),
        P("tp"),
        P(None, None, "tp"),
        P("tp", None),
        P(("grp", "tok", "tp"), None),
        P(),
        P(),
    )
    return jax.shard_map(
        on_device,
        mesh=mesh,
        in_specs=placed,
        out_specs=(P(), P(("grp", "tok", "tp"), None), P(("grp", "tok", "tp"), None)),
        check_vma=False,
    )
```

```python
import functools
import math

import jax
import jax.numpy as jnp
from jax import lax
from jax.experimental import pallas as pl
from jax.experimental.pallas import tpu as pltpu
from jax.sharding import PartitionSpec as P

HD = 128
EXP2_SCALE = math.log2(math.e) / math.sqrt(HD)
MESH = pl.DeviceIdType.MESH
BF16, F32 = jnp.bfloat16, jnp.float32

FIRSTS = ("x", "z", "x", "z", "x", "z", "x", "z", "x", "z", "x", "z")
N_X = 8
STUDENT = (N_X, N_X + 1)
PRED = (N_X + 2, N_X + 3)
NAMES_X = ("z0", "z1", "z2", "z3", "r0", "l0", "r1", "l1", "fr0", "fr1", "fl0", "fl1")
NAMES_K = ("s0", "s1", "s2", "s3", "u0", "d0", "fu", "fd")


def make_plan():
    n = N_X
    plan = [("x0", 0), ("g",), ("x0", 1), ("x0", 2), ("prep",), ("x1", 0)]
    for c in range(n):
        plan.append(("x2", c))
        if c + 3 <= STUDENT[1]:
            plan.append(("x0", c + 3))
        plan.append(("x1", c + 1))
        if c >= 1:
            plan.append(("k1", c - 1))
        if c >= 2:
            plan.append(("k3", c - 2))
            if c % 2 == 0 and c > 2:
                plan.append(("ks", c // 2 - 1, 0, c - 2))
            plan.append(("qs", 0, c // 2, c - 2))
        if c >= 1:
            plan.append(("k2", c - 1))
        plan += [("x3", c), ("p", c)]
    pair, half = n // 2 - 1, n // 2 - 1
    plan += [
        ("x2", n), ("x1", n + 1), ("ks", pair, 0, half), ("k1", n - 1), ("x2", n + 1),
        ("ks", pair, half, n - 2), ("k2", n - 1), ("k3", n - 2), ("qs", 0, n // 2, n - 2),
        ("x3", n), ("x3", n + 1), ("act",), ("k3", n - 1),
    ]
    return tuple(plan)


PLAN = make_plan()


def whole_kernel(
    sizes, teacher_in, gain, w_hbm, probe, student, up_hbm, down_hbm,
    loss, up_out, down_out,
    xb, gains, w, normed, qb, kvb, top_s, sum_s, acc_s,
    up_raw, up, down, act, slope,
    tx_a, rx_a, tz_a, rz_a, tx_b, rx_b, tz_b, rz_b, part_a, part_b,
    acc_down, acc_up, core_down, core_up, mine_down, mine_up,
    sent_down, sent_up, got_down, got_up, up_rows, up_got,
    loss_tp, loss_core, loss_gy,
    xs, xr, gs, gr, ks, kr, local, fs, fr,
    lt_s, lt_r, co_s, co_r, gy_s, gy_r, aa_s, aa_r,
):
    grps, toks, tps = sizes
    xn, ys = tps // 2, toks // 2
    gys = grps * ys
    grp, tok, tp = lax.axis_index("grp"), lax.axis_index("tok"), lax.axis_index("tp")
    chunk, feat = xb.shape[2], xb.shape[3]
    half = chunk // 2
    width = qb.shape[2]
    heads = width // HD
    pair = 2 * chunk
    zh, x = lax.rem(tp, 2), tp // 2
    core, y = lax.rem(tok, 2), tok // 2
    gy = grp * ys + y
    zp = tp + 1 - 2 * zh

    def along_x(d):
        return lax.rem(x + d, xn) * 2 + zh

    def along_y(d):
        return lax.rem(y + d, ys) * 2 + core

    def other(slot):
        return slot + 1 - 2 * zh

    def tp_peer(d):
        return lax.rem(tp + d, tps)

    def gy_peer(d):
        return lax.rem(gy + d, gys)

    def at_tp(to):
        return (grp, tok, to)

    def at_gy(to):
        return (to // ys, lax.rem(to, ys) * 2 + core, tp)

    right, left, across = along_x(1), along_x(3), along_x(2)
    above, below, yfar = along_y(1), along_y(3), along_y(2)
    to_z, to_right, to_left = at_tp(zp), at_tp(right), at_tp(left)
    to_up, to_down = (grp, above, tp), (grp, below, tp)
    to_sib = (grp, tok + 1 - 2 * core, tp)

    fetch = [
        pltpu.make_async_copy(w_hbm, w, local.at[0]),
        pltpu.make_async_copy(up_hbm, up_raw, local.at[1]),
        pltpu.make_async_copy(down_hbm.at[:, tp], down, local.at[2]),
    ]
    keep = [
        pltpu.make_async_copy(
            teacher_in.at[pl.ds(c * chunk, chunk), :], xb.at[c, tp], local.at[3 + c]
        )
        for c in range(N_X)
    ] + [
        pltpu.make_async_copy(
            student.at[:, pl.ds(i * feat, feat)], xb.at[c, tp], local.at[3 + c]
        )
        for i, c in enumerate(STUDENT)
    ]
    for copy in keep + fetch:
        copy.start()
    gains[tp] = gain[...]

    barrier = pltpu.get_barrier_semaphore()
    greet = [at_tp(tp_peer(d)) for d in range(1, tps)]
    greet += [at_gy(gy_peer(d)) for d in range(1, gys)] + [to_sib]
    for device in greet:
        pl.semaphore_signal(barrier, inc=1, device_id=device, device_id_type=MESH)
    pl.semaphore_wait(barrier, len(greet))

    sent = {}

    def send(name, src, dst, ssem, rsem, device):
        copy = pltpu.make_async_remote_copy(
            src_ref=src, dst_ref=dst, send_sem=ssem, recv_sem=rsem,
            device_id=device, device_id_type=MESH,
        )
        copy.start()
        sent[name] = copy

    def arrived(*names):
        for name in names:
            sent[name].wait_recv()


    def send_x(name, c, ref, device):
        i = NAMES_X.index(name)
        send((name, c), ref[0], ref[1], xs.at[c, i], xr.at[c, i], device)

    def own(c):
        to = xb.at[c, tp]
        if c < N_X:
            return teacher_in.at[pl.ds(c * chunk, chunk), :], to
        if c in STUDENT:
            return student.at[:, pl.ds((c - N_X) * feat, feat)], to
        return to, to

    def slot(c, p):
        return xb.at[c, p], xb.at[c, p]

    def part(c, p, h):
        ref = xb.at[c, p, pl.ds(h * half, half), :]
        return ref, ref

    def x0(c):
        if FIRSTS[c] == "z":
            send_x("z0", c, own(c), to_z)
        send_x("r0", c, own(c), to_right)
        send_x("l0", c, own(c), to_left)
        if FIRSTS[c] == "x":
            send_x("z0", c, own(c), to_z)

    def x1(c):
        if FIRSTS[c] == "z":
            arrived(("z0", c))
            send_x("r1", c, slot(c, zp), to_right)
            send_x("l1", c, slot(c, zp), to_left)
        else:
            arrived(("r0", c))
            send_x("fr0", c, part(c, left, 0), to_right)
            send_x("z1", c, slot(c, left), to_z)
            arrived(("l0", c))
            send_x("fl0", c, part(c, right, 1), to_left)
            send_x("z2", c, slot(c, right), to_z)

    def x2(c):
        if FIRSTS[c] == "z":
            arrived(("r0", c))
            send_x("fr0", c, part(c, left, 0), to_right)
            arrived(("l0", c))
            send_x("fl0", c, part(c, right, 1), to_left)
            arrived(("r1", c))
            send_x("fr1", c, part(c, other(left), 0), to_right)
            arrived(("l1", c))
            send_x("fl1", c, part(c, other(right), 1), to_left)
        else:
            arrived(("fr0", c), ("fl0", c))
            send_x("z3", c, slot(c, across), to_z)

    def x3(c):
        if FIRSTS[c] == "z":
            arrived(("fr0", c), ("fl0", c), ("fr1", c), ("fl1", c))
        else:
            arrived(("z0", c), ("z1", c), ("z2", c), ("z3", c))

    def greetings():
        for d in range(1, tps):
            send(("g", d), gains.at[tp], gains.at[tp], gs.at[d], gr.at[d], at_tp(tp_peer(d)))
        top_s[...] = jnp.full(top_s.shape, -1e30, F32)
        sum_s[...] = jnp.zeros(sum_s.shape, F32)
        acc_s[...] = jnp.zeros(acc_s.shape, F32)

    def prepare():
        fetch[1].wait()
        ff, units = up_raw.shape[1], up.shape[1]
        piece = units // (2 * gys)
        step = 512
        total = jnp.zeros(up.shape, F32)
        for b in range(ff // step):
            row = lax.broadcasted_iota(jnp.int32, (step, units), 0) + b * step
            col = lax.broadcasted_iota(jnp.int32, (step, units), 1)
            rest = jnp.bitwise_and(col, piece - 1)
            unit = (col - rest) * tps + tp * piece + rest
            pick = jnp.where(row == unit, 1.0, 0.0).astype(BF16)
            total = total + jnp.dot(
                up_raw[:, b * step : (b + 1) * step], pick, preferred_element_type=F32
            )
        up[...] = total.astype(BF16)
        fetch[0].wait()
        fetch[2].wait()
        for d in range(1, tps):
            arrived(("g", d))


    def send_k(name, c, ref, device):
        i = NAMES_K.index(name)
        send((name, c), ref, ref, ks.at[c, i], kr.at[c, i], device)

    def project(c):
        keep[c].wait()
        step = 64

        def rows_of(i, _):
            rows = pl.ds(pl.multiple_of(i * step, step), step)
            squares = jnp.zeros((step, feat), F32)
            for p in range(tps):
                some = xb[c, p, rows, :].astype(F32)
                squares = squares + some * some
            mean = jnp.sum(squares, axis=1, keepdims=True) / (tps * feat)
            scale = lax.rsqrt(mean + 1e-05)
            for p in range(tps):
                some = xb[c, p, rows, :].astype(F32)
                normed[rows, p * feat : (p + 1) * feat] = (
                    some * scale * gains[p, 0:1, :]
                ).astype(BF16)
            return 0

        lax.fori_loop(0, chunk // step, rows_of, 0)
        for j in (1, 2):
            kvb[c, tok, :, (j - 1) * width : j * width] = jnp.dot(
                normed[...], w[j], preferred_element_type=F32
            ).astype(BF16)
        send_k("u0", c, kvb.at[c, tok], to_up)
        send_k("d0", c, kvb.at[c, tok], to_down)
        send_k("s0", c, kvb.at[c, tok], to_sib)
        qb[c] = jnp.dot(normed[...], w[0], preferred_element_type=F32).astype(BF16)

    def k1(c):
        arrived(("u0", c))
        send_k("fu", c, kvb.at[c, below, pl.ds(0, half), :], to_up)
        send_k("s1", c, kvb.at[c, below], to_sib)
        arrived(("d0", c))
        send_k("fd", c, kvb.at[c, above, pl.ds(half, half), :], to_down)
        send_k("s2", c, kvb.at[c, above], to_sib)

    def k2(c):
        arrived(("fu", c), ("fd", c))
        send_k("s3", c, kvb.at[c, yfar], to_sib)

    def k3(c):
        arrived(("s0", c), ("s1", c), ("s2", c), ("s3", c))

    def attend(i, c):
        result = []
        for head in range(heads):
            cols = slice(head * HD, (head + 1) * HD)
            vcols = slice(width + head * HD, width + (head + 1) * HD)
            query = qb[pl.ds(2 * i, 2), :, cols].reshape(pair, HD)
            top = top_s[i, head][:, :1]
            keys = kvb[c, :, :, cols].reshape(toks * chunk, HD)
            values = kvb[c, :, :, vcols].reshape(toks * chunk, HD)
            scores = lax.dot_general(
                query, keys, (((1,), (1,)), ((), ())), preferred_element_type=F32
            )
            top_new = jnp.maximum(top, jnp.max(scores, axis=1, keepdims=True))
            fade = jnp.exp2((top - top_new) * EXP2_SCALE)
            weights = jnp.exp2(scores * EXP2_SCALE - top_new * EXP2_SCALE).astype(BF16)
            both = jnp.concatenate([values, jnp.ones_like(values)], axis=1)
            res = jnp.dot(weights, both, preferred_element_type=F32)
            result.append(
                (top_new, sum_s[i, head] * fade + res[:, HD:], acc_s[i, head] * fade + res[:, :HD])
            )
        return result

    def attend_keep(i, c):
        for head, (top, total, acc) in enumerate(attend(i, c)):
            top_s[i, head] = jnp.broadcast_to(top, (pair, HD))
            sum_s[i, head] = total
            acc_s[i, head] = acc
        return 0

    def queries(lo, hi, c):
        lax.fori_loop(lo, hi, lambda i, _: attend_keep(i, c), 0)

    def keys(i, lo, hi):
        lax.fori_loop(lo, hi, lambda c, _: attend_keep(i, c), 0)

    def activate():
        for c in STUDENT:
            keep[c].wait()

        def rows_of(i, _):
            rows = pl.ds(pl.multiple_of(i * pair, pair), pair)
            hidden = jnp.zeros((pair, up.shape[1]), F32)
            for j, c in enumerate(STUDENT):
                some = xb[c, pl.ds(2 * i, 2)].reshape(pair, feat)
                hidden = hidden + jnp.dot(
                    some, up[j * feat : (j + 1) * feat, :], preferred_element_type=F32
                )
            rate = math.sqrt(2 / math.pi)
            square = hidden * hidden
            tanh = jnp.tanh(rate * (hidden + 0.044715 * (hidden * square)))
            cdf = 0.5 * (1.0 + tanh)
            act[rows, :] = (hidden * cdf).astype(BF16)
            slope[rows, :] = cdf + 0.5 * hidden * (1.0 - tanh * tanh) * (
                rate * (1.0 + 3 * 0.044715 * square)
            )
            return 0

        lax.fori_loop(0, xn, rows_of, 0)

    steps = dict(
        x0=x0, x1=x1, x2=x2, x3=x3, p=project, k1=k1, k2=k2, k3=k3,
        qs=queries, ks=keys, g=greetings, prep=prepare, act=activate,
    )
    for step in PLAN:
        steps[step[0]](*step[1:])

    down_full = down[...].reshape(act.shape[1], 2 * feat)

    def block_out(k):
        i = lax.rem(x + k, xn)
        feats = jnp.concatenate(
            [(acc / total).astype(BF16) for _, total, acc in attend(i, N_X - 1)], axis=1
        )
        rows = pl.ds(pl.multiple_of(i * pair, pair), pair)
        diff = jnp.dot(act[rows, :], down_full, preferred_element_type=F32) - jnp.dot(
            feats, probe[...], preferred_element_type=F32
        )
        diff = diff.reshape(2, chunk, 2 * feat)
        part_b[k] = diff[:, :, feat:]
        tz_b[k] = part_b[k, 1 - zh].astype(BF16)
        send(("zb", k), tz_b.at[k], rz_b.at[k], fs.at[0, k], fr.at[0, k], to_z)
        if k == 0:
            part_a[...] = diff[:, :, :feat]
        else:
            tx_a[k] = diff[:, :, :feat].astype(BF16)
            send(("xa", k), tx_a.at[k], rx_a.at[k], fs.at[1, k], fr.at[1, k], at_tp(along_x(k)))

    def forward(k):
        arrived(("zb", k))
        some = part_b[k, zh] + rz_b[k].astype(F32)
        if k == 0:
            return some
        tx_b[k] = some.astype(BF16)
        send(("xb", k), tx_b.at[k], rx_b.at[k], fs.at[2, k], fr.at[2, k], at_tp(along_x(k)))

    block_out(1)
    block_out(2)
    forward(1)
    block_out(3)
    forward(2)
    block_out(0)
    forward(3)
    arrived(("xa", 1), ("xa", 2), ("xa", 3))
    part_a[...] = part_a[...] + sum(rx_a[k].astype(F32) for k in range(1, xn))
    tz_a[...] = part_a[1 - zh].astype(BF16)
    send("za", tz_a, rz_a, fs.at[3, 0], fr.at[3, 0], to_z)
    diff_b = forward(0)
    arrived(("xb", 1), ("xb", 2), ("xb", 3))
    diff_b = diff_b + sum(rx_b[k].astype(F32) for k in range(1, xn))
    grad_scale = 1.0 / math.sqrt(chunk * tps * toks * grps)
    xb[PRED[1], tp] = (diff_b * grad_scale).astype(BF16)
    x0(PRED[1])
    arrived("za")
    diff_a = part_a[zh] + rz_a[...].astype(F32)
    xb[PRED[0], tp] = (diff_a * grad_scale).astype(BF16)
    x0(PRED[0])
    squares = jnp.sum((diff_a * diff_a + diff_b * diff_b).reshape(chunk // 8, 8, feat), axis=0)
    loss_tp[tp] = sum(squares[:, i * 128 : (i + 1) * 128] for i in range(feat // 128))
    for d in range(1, tps):
        send(("lt", d), loss_tp.at[tp], loss_tp.at[tp], lt_s.at[d], lt_r.at[d], at_tp(tp_peer(d)))
    x1(PRED[1])
    x1(PRED[0])
    x2(PRED[1])
    x2(PRED[0])
    x3(PRED[1])

    def pred(c):
        return xb[c].reshape(tps * chunk, feat)

    def grad_down_of(i):
        acc_down[:, :, :, i * feat : (i + 1) * feat] = lax.dot_general(
            act[...], pred(PRED[i]), (((0,), (0,)), ((), ())), preferred_element_type=F32
        ).reshape(gys, 2, -1, feat)

    def d_act_of(i):
        return lax.dot_general(
            pred(PRED[i]), down_full[:, i * feat : (i + 1) * feat],
            (((1,), (1,)), ((), ())), preferred_element_type=F32,
        )

    grad_down_of(1)
    d_act = d_act_of(1)
    x3(PRED[0])
    grad_down_of(0)
    for d in range(1, tps):
        arrived(("lt", d))
    loss_core[core] = sum(loss_tp[i] for i in range(tps))
    send("cd", acc_down.at[:, 1 - core], core_down, co_s.at[0], co_r.at[0], to_sib)
    send("cl", loss_core.at[core], loss_core.at[core], co_s.at[1], co_r.at[1], to_sib)
    d_act = d_act + d_act_of(0)
    d_hidden = (d_act * slope[...]).astype(BF16)
    for i, c in enumerate(STUDENT):
        acc_up[i * gys // 2 : (i + 1) * gys // 2] = lax.dot_general(
            xb[c].reshape(tps * chunk, feat), d_hidden,
            (((0,), (0,)), ((), ())), preferred_element_type=F32,
        ).reshape(gys // 2, 2, -1, act.shape[1])
    send("cu", acc_up.at[:, 1 - core], core_up, co_s.at[2], co_r.at[2], to_sib)

    arrived("cd", "cl")
    mine_down[...] = acc_down[:, core] + core_down[...]
    sent_down[...] = mine_down[...].astype(BF16)
    loss_gy[gy] = loss_core[0] + loss_core[1]
    for d in range(1, gys):
        to = gy_peer(d)
        send(("gd", d), sent_down.at[to], got_down.at[d], gy_s.at[0, d], gy_r.at[0, d], at_gy(to))
        send(("gl", d), loss_gy.at[gy], loss_gy.at[gy], gy_s.at[1, d], gy_r.at[1, d], at_gy(to))
    arrived("cu")
    mine_up[...] = acc_up[:, core] + core_up[...]
    sent_up[...] = mine_up[...].astype(BF16)
    for d in range(1, gys):
        to = gy_peer(d)
        send(("gu", d), sent_up.at[to], got_up.at[d], gy_s.at[2, d], gy_r.at[2, d], at_gy(to))
    total = mine_up[gy]
    for d in range(1, gys):
        arrived(("gu", d))
    for d in range(1, gys):
        total = total + got_up[d].astype(F32)
    up_rows[...] = total.reshape(up_rows.shape)
    for d in range(1, tps):
        q = tp_peer(d)
        send(("aa", d), up_rows.at[q], up_got.at[tp], aa_s.at[d], aa_r.at[d], at_tp(q))
    for d in range(1, gys):
        arrived(("gd", d), ("gl", d))
    total = mine_down[gy]
    for d in range(1, gys):
        total = total + got_down[d].astype(F32)
    down_out[...] = total
    loss[...] = sum(loss_gy[i] for i in range(gys))
    up_got[tp] = up_rows[tp]
    for d in range(1, tps):
        arrived(("aa", d))
    up_out[...] = up_got[...]
    for copy in sent.values():
        copy.wait_send()


def on_device(teacher_in, norm_gain, w_qkv, probe, student_in, w_up, w_down):
    grps, toks, tps = sizes = tuple(lax.axis_size(name) for name in ("grp", "tok", "tp"))
    gys, xn = grps * toks // 2, tps // 2
    rows, feat = teacher_in.shape
    depth, _, width = w_qkv.shape
    ff, ds = w_down.shape
    heads, units, chunk = width // HD, ff // tps, rows // N_X
    piece, strip = units // (2 * gys), ds // (2 * gys)
    gain = jnp.broadcast_to(norm_gain.astype(F32)[None, :], (8, feat))
    dma = pltpu.SemaphoreType.DMA
    vmem, hbm = pl.BlockSpec(memory_space=pltpu.VMEM), pl.BlockSpec(memory_space=pl.ANY)
    state = pltpu.VMEM((N_X // 2, heads, 2 * chunk, HD), F32)
    squares, grad_up, grad_down = pl.pallas_call(
        functools.partial(whole_kernel, sizes),
        name="distill",
        out_shape=(
            jax.ShapeDtypeStruct((8, 128), F32),
            jax.ShapeDtypeStruct((tps, strip // tps, units), F32),
            jax.ShapeDtypeStruct((piece, ds), F32),
        ),
        in_specs=[vmem, vmem, hbm, vmem, vmem, hbm, hbm],
        out_specs=[vmem] * 3,
        scratch_shapes=[
            pltpu.VMEM((len(FIRSTS), tps, chunk, feat), BF16),
            pltpu.VMEM((tps, 8, feat), F32),
            pltpu.VMEM((3, depth, width), BF16),
            pltpu.VMEM((chunk, depth), BF16),
            pltpu.VMEM((N_X, chunk, width), BF16),
            pltpu.VMEM((N_X, toks, chunk, 2 * width), BF16),
            state, state, state,
            pltpu.VMEM((ds, ff), BF16),
            pltpu.VMEM((ds, units), BF16),
            pltpu.VMEM((2 * gys, piece, ds), BF16),
            pltpu.VMEM((rows, units), BF16),
            pltpu.VMEM((rows, units), F32),
            pltpu.VMEM((xn, 2, chunk, feat), BF16),
            pltpu.VMEM((xn, 2, chunk, feat), BF16),
            pltpu.VMEM((chunk, feat), BF16),
            pltpu.VMEM((chunk, feat), BF16),
            pltpu.VMEM((xn, chunk, feat), BF16),
            pltpu.VMEM((xn, chunk, feat), BF16),
            pltpu.VMEM((xn, chunk, feat), BF16),
            pltpu.VMEM((xn, chunk, feat), BF16),
            pltpu.VMEM((2, chunk, feat), F32),
            pltpu.VMEM((xn, 2, chunk, feat), F32),
            pltpu.VMEM((gys, 2, piece, ds), F32),
            pltpu.VMEM((gys, 2, strip, units), F32),
            pltpu.VMEM((gys, piece, ds), F32),
            pltpu.VMEM((gys, strip, units), F32),
            pltpu.VMEM((gys, piece, ds), F32),
            pltpu.VMEM((gys, strip, units), F32),
            pltpu.VMEM((gys, piece, ds), BF16),
            pltpu.VMEM((gys, strip, units), BF16),
            pltpu.VMEM((gys, piece, ds), BF16),
            pltpu.VMEM((gys, strip, units), BF16),
            pltpu.VMEM((tps, strip // tps, units), F32),
            pltpu.VMEM((tps, strip // tps, units), F32),
            pltpu.VMEM((tps, 8, 128), F32),
            pltpu.VMEM((2, 8, 128), F32),
            pltpu.VMEM((gys, 8, 128), F32),
            dma((len(FIRSTS), len(NAMES_X))), dma((len(FIRSTS), len(NAMES_X))),
            dma((tps,)), dma((tps,)),
            dma((N_X, len(NAMES_K))), dma((N_X, len(NAMES_K))),
            dma((3 + PRED[0],)), dma((4, xn)), dma((4, xn)),
            dma((tps,)), dma((tps,)), dma((3,)), dma((3,)),
            dma((3, gys)), dma((3, gys)), dma((tps,)), dma((tps,)),
        ],
        compiler_params=pltpu.CompilerParams(
            collective_id=1, has_side_effects=True, vmem_limit_bytes=61 << 20
        ),
    )(
        teacher_in, gain, jnp.transpose(w_qkv, (1, 0, 2)), probe, student_in, w_up,
        w_down.reshape(2 * gys, tps, piece, ds),
    )
    grad_up = grad_up.reshape(tps, -1, 2 * gys, piece).transpose(1, 2, 0, 3).reshape(-1, ff)
    loss = jnp.sum(squares) / (chunk * tps * toks * grps * ds)
    return (loss, grad_up, grad_down)


def solution(mesh):
    placed = (
        P(("grp", "tok"), "tp"),
        P("tp"),
        P(None, None, "tp"),
        P("tp", None),
        P(("grp", "tok", "tp"), None),
        P(),
        P(),
    )
    return jax.shard_map(
        on_device,
        mesh=mesh,
        in_specs=placed,
        out_specs=(P(), P(("grp", "tok", "tp"), None), P(("grp", "tok", "tp"), None)),
        check_vma=False,
    )
```

```python
import functools
import math

import jax
import jax.numpy as jnp
from jax import lax
from jax.experimental import pallas as pl
from jax.experimental.pallas import tpu as pltpu
from jax.sharding import PartitionSpec as P

HD = 128
EXP2_SCALE = math.log2(math.e) / math.sqrt(HD)
MESH = pl.DeviceIdType.MESH
BF16, F32 = jnp.bfloat16, jnp.float32

FIRSTS = ("x", "z") * 7
N_X = 8
STUDENT = (N_X, N_X + 1)
PROBE = (N_X + 2, N_X + 3)
PRED = (N_X + 4, N_X + 5)
NAMES_X = ("z0", "z1", "z2", "z3", "r0", "l0", "r1", "l1", "fr0", "fr1", "fl0", "fl1")
NAMES_K = ("s0", "s1", "s2", "s3", "u0", "d0", "fu", "fd")


def make_plan(early=3):
    n, last = N_X, PROBE[1]
    plan = [("x0", 0), ("g",)] + [("x0", c) for c in range(1, early)]
    plan += [("prep",), ("x1", 0), ("x1", 1), ("x2", 0), ("pred",)]
    for c in range(n):
        plan += [("x0", c + early)] if c + early <= last else []
        plan += [("x1", c + 2), ("x2", c + 1)]
        if c >= 2:
            plan.append(("k2", c - 2))
        if c >= 3:
            plan.append(("k3", c - 3))
            if c % 2 == 0:
                plan.append(("ks", c // 2 - 1, 0, c - 3))
            plan.append(("qs", 0, c // 2, c - 3))
        if c >= 1:
            plan.append(("k1", c - 1))
        plan += [("x3", c), ("p", c)]
    plan += [("x0", c) for c in range(n + early, last + 1)]
    pair = n // 2 - 1
    plan += [
        ("k2", n - 2), ("ks", pair, 0, 2), ("x2", n + 1), ("x1", n + 2), ("ks", pair, 2, n - 3),
        ("k1", n - 1), ("x1", n + 3), ("x2", n + 2), ("k3", n - 3), ("qs", 0, n // 2, n - 3),
        ("k2", n - 1), ("x2", n + 3), ("x3", n), ("x3", n + 1), ("act",),
        ("k3", n - 2), ("x3", n + 2), ("x3", n + 3), ("share",), ("qs", 0, n // 2, n - 2),
        ("k3", n - 1),
    ]
    return tuple(plan)


PLAN = make_plan()


def whole_kernel(
    sizes, teacher_in, gain, w_hbm, probe, student, up_hbm, down_hbm,
    loss, up_out, down_out,
    xb, gains, w, normed, qb, kvb, top_s, sum_s, acc_s,
    up_raw, up, down_raw, act, slope, out_pred, feats_out, feats_in, probe_sib,
    acc_down, acc_up, core_down, core_up, mine_down, mine_up,
    sent_down, sent_up, got_down, got_up, up_rows, up_got,
    loss_tp, loss_core, loss_gy,
    xs, xr, gs, gr, ks, kr, local, fs, fr, ps, pr,
    lt_s, lt_r, co_s, co_r, gy_s, gy_r, aa_s, aa_r,
):
    grps, toks, tps = sizes
    xn, ys = tps // 2, toks // 2
    gys = grps * ys
    grp, tok, tp = lax.axis_index("grp"), lax.axis_index("tok"), lax.axis_index("tp")
    chunk, feat = xb.shape[2], xb.shape[3]
    half = chunk // 2
    width = qb.shape[2]
    heads = width // HD
    pair = 2 * chunk
    zh, x = lax.rem(tp, 2), tp // 2
    core, y = lax.rem(tok, 2), tok // 2
    gy = grp * ys + y
    zp = tp + 1 - 2 * zh

    def along_x(d):
        return lax.rem(x + d, xn) * 2 + zh

    def along_y(d):
        return lax.rem(y + d, ys) * 2 + core

    def other(slot):
        return slot + 1 - 2 * zh

    def tp_peer(d):
        return lax.rem(tp + d, tps)

    def gy_peer(d):
        return lax.rem(gy + d, gys)

    def at_tp(to):
        return (grp, tok, to)

    def at_gy(to):
        return (to // ys, lax.rem(to, ys) * 2 + core, tp)

    right, left, across = along_x(1), along_x(3), along_x(2)
    above, below, yfar = along_y(1), along_y(3), along_y(2)
    to_z, to_right, to_left = at_tp(zp), at_tp(right), at_tp(left)
    to_up, to_down = (grp, above, tp), (grp, below, tp)
    to_sib = (grp, tok + 1 - 2 * core, tp)

    def own_probe(i):
        return probe.at[pl.ds(pl.multiple_of(core * chunk, chunk), chunk), pl.ds(i * feat, feat)]

    fetch = [
        pltpu.make_async_copy(w_hbm, w, local.at[0]),
        pltpu.make_async_copy(up_hbm, up_raw, local.at[1]),
        pltpu.make_async_copy(down_hbm, down_raw, local.at[2]),
    ]
    keep = [
        pltpu.make_async_copy(
            teacher_in.at[pl.ds(c * chunk, chunk), :], xb.at[c, tp], local.at[3 + c]
        )
        for c in range(N_X)
    ] + [
        pltpu.make_async_copy(
            student.at[:, pl.ds(i * feat, feat)], xb.at[c, tp], local.at[3 + c]
        )
        for i, c in enumerate(STUDENT)
    ] + [
        pltpu.make_async_copy(own_probe(i), xb.at[c, tp], local.at[3 + c])
        for i, c in enumerate(PROBE)
    ]
    for copy in keep + fetch:
        copy.start()
    gains[tp] = gain[...]

    barrier = pltpu.get_barrier_semaphore()
    greet = [at_tp(tp_peer(d)) for d in range(1, tps)]
    greet += [at_gy(gy_peer(d)) for d in range(1, gys)] + [to_sib]
    for device in greet:
        pl.semaphore_signal(barrier, inc=1, device_id=device, device_id_type=MESH)
    pl.semaphore_wait(barrier, len(greet))

    sent = {}

    def send(name, src, dst, ssem, rsem, device):
        copy = pltpu.make_async_remote_copy(
            src_ref=src, dst_ref=dst, send_sem=ssem, recv_sem=rsem,
            device_id=device, device_id_type=MESH,
        )
        copy.start()
        sent[name] = copy

    def arrived(*names):
        for name in names:
            sent[name].wait_recv()


    def send_x(name, c, ref, device):
        i = NAMES_X.index(name)
        send((name, c), ref[0], ref[1], xs.at[c, i], xr.at[c, i], device)

    def own(c):
        to = xb.at[c, tp]
        if c < N_X:
            return teacher_in.at[pl.ds(c * chunk, chunk), :], to
        if c in STUDENT:
            return student.at[:, pl.ds((c - N_X) * feat, feat)], to
        if c in PROBE:
            return own_probe(c - PROBE[0]), to
        return to, to

    def slot(c, p):
        return xb.at[c, p], xb.at[c, p]

    def part(c, p, h):
        ref = xb.at[c, p, pl.ds(h * half, half), :]
        return ref, ref

    def x0(c):
        if FIRSTS[c] == "z":
            send_x("z0", c, own(c), to_z)
        send_x("r0", c, own(c), to_right)
        send_x("l0", c, own(c), to_left)
        if FIRSTS[c] == "x":
            send_x("z0", c, own(c), to_z)

    def x1(c):
        if FIRSTS[c] == "z":
            arrived(("z0", c))
            send_x("r1", c, slot(c, zp), to_right)
            send_x("l1", c, slot(c, zp), to_left)
        else:
            arrived(("r0", c))
            send_x("fr0", c, part(c, left, 0), to_right)
            send_x("z1", c, slot(c, left), to_z)
            arrived(("l0", c))
            send_x("fl0", c, part(c, right, 1), to_left)
            send_x("z2", c, slot(c, right), to_z)

    def x2(c):
        if FIRSTS[c] == "z":
            arrived(("r0", c))
            send_x("fr0", c, part(c, left, 0), to_right)
            arrived(("l0", c))
            send_x("fl0", c, part(c, right, 1), to_left)
            arrived(("r1", c))
            send_x("fr1", c, part(c, other(left), 0), to_right)
            arrived(("l1", c))
            send_x("fl1", c, part(c, other(right), 1), to_left)
        else:
            arrived(("fr0", c), ("fl0", c))
            send_x("z3", c, slot(c, across), to_z)

    def x3(c):
        if FIRSTS[c] == "z":
            arrived(("fr0", c), ("fl0", c), ("fr1", c), ("fl1", c))
        else:
            arrived(("z0", c), ("z1", c), ("z2", c), ("z3", c))

    def greetings():
        for d in range(1, tps):
            send(("g", d), gains.at[tp], gains.at[tp], gs.at[d], gr.at[d], at_tp(tp_peer(d)))
        top_s[...] = jnp.full(top_s.shape, -1e30, F32)
        sum_s[...] = jnp.zeros(sum_s.shape, F32)
        acc_s[...] = jnp.zeros(acc_s.shape, F32)

    def prepare():
        fetch[1].wait()
        ff, units = up_raw.shape[1], up.shape[1]
        piece = units // (2 * gys)
        step = 512
        total = jnp.zeros(up.shape, F32)
        for b in range(ff // step):
            row = lax.broadcasted_iota(jnp.int32, (step, units), 0) + b * step
            col = lax.broadcasted_iota(jnp.int32, (step, units), 1)
            rest = jnp.bitwise_and(col, piece - 1)
            unit = (col - rest) * tps + tp * piece + rest
            pick = jnp.where(row == unit, 1.0, 0.0).astype(BF16)
            total = total + jnp.dot(
                up_raw[:, b * step : (b + 1) * step], pick, preferred_element_type=F32
            )
        up[...] = total.astype(BF16)
        fetch[0].wait()
        fetch[2].wait()
        for d in range(1, tps):
            arrived(("g", d))


    def send_k(name, c, ref, device):
        i = NAMES_K.index(name)
        send((name, c), ref, ref, ks.at[c, i], kr.at[c, i], device)

    def project(c):
        keep[c].wait()
        step = 64

        def rows_of(i, _):
            rows = pl.ds(pl.multiple_of(i * step, step), step)
            squares = jnp.zeros((step, feat), F32)
            for p in range(tps):
                some = xb[c, p, rows, :].astype(F32)
                squares = squares + some * some
            mean = jnp.sum(squares, axis=1, keepdims=True) / (tps * feat)
            scale = lax.rsqrt(mean + 1e-05)
            for p in range(tps):
                some = xb[c, p, rows, :].astype(F32)
                normed[rows, p * feat : (p + 1) * feat] = (
                    some * scale * gains[p, 0:1, :]
                ).astype(BF16)
            return 0

        lax.fori_loop(0, chunk // step, rows_of, 0)
        for j in (1, 2):
            kvb[c, tok, :, (j - 1) * width : j * width] = jnp.dot(
                normed[...], w[j], preferred_element_type=F32
            ).astype(BF16)
        send_k("u0", c, kvb.at[c, tok], to_up)
        send_k("d0", c, kvb.at[c, tok], to_down)
        send_k("s0", c, kvb.at[c, tok], to_sib)
        qb[c] = jnp.dot(normed[...], w[0], preferred_element_type=F32).astype(BF16)

    def k1(c):
        arrived(("u0", c))
        send_k("fu", c, kvb.at[c, below, pl.ds(0, half), :], to_up)
        send_k("s1", c, kvb.at[c, below], to_sib)
        arrived(("d0", c))
        send_k("fd", c, kvb.at[c, above, pl.ds(half, half), :], to_down)
        send_k("s2", c, kvb.at[c, above], to_sib)

    def k2(c):
        arrived(("fu", c), ("fd", c))
        send_k("s3", c, kvb.at[c, yfar], to_sib)

    def k3(c):
        arrived(("s0", c), ("s1", c), ("s2", c), ("s3", c))

    def attend(i, c):
        result = []
        for head in range(heads):
            cols = slice(head * HD, (head + 1) * HD)
            vcols = slice(width + head * HD, width + (head + 1) * HD)
            query = qb[pl.ds(2 * i, 2), :, cols].reshape(pair, HD)
            top = top_s[i, head][:, :1]
            keys = kvb[c, :, :, cols].reshape(toks * chunk, HD)
            values = kvb[c, :, :, vcols].reshape(toks * chunk, HD)
            scores = lax.dot_general(
                query, keys, (((1,), (1,)), ((), ())), preferred_element_type=F32
            )
            top_new = jnp.maximum(top, jnp.max(scores, axis=1, keepdims=True))
            fade = jnp.exp2((top - top_new) * EXP2_SCALE)
            weights = jnp.exp2(scores * EXP2_SCALE - top_new * EXP2_SCALE).astype(BF16)
            both = jnp.concatenate([values, jnp.ones_like(values)], axis=1)
            res = jnp.dot(weights, both, preferred_element_type=F32)
            result.append(
                (top_new, sum_s[i, head] * fade + res[:, HD:], acc_s[i, head] * fade + res[:, :HD])
            )
        return result

    def attend_keep(i, c):
        for head, (top, total, acc) in enumerate(attend(i, c)):
            top_s[i, head] = jnp.broadcast_to(top, (pair, HD))
            sum_s[i, head] = total
            acc_s[i, head] = acc
        return 0

    def queries(lo, hi, c):
        lax.fori_loop(lo, hi, lambda i, _: attend_keep(i, c), 0)

    def keys(i, lo, hi):
        lax.fori_loop(lo, hi, lambda c, _: attend_keep(i, c), 0)

    def gelu(hidden):
        rate = math.sqrt(2 / math.pi)
        square = hidden * hidden
        tanh = jnp.tanh(rate * (hidden + 0.044715 * (hidden * square)))
        cdf = 0.5 * (1.0 + tanh)
        rise = cdf + 0.5 * hidden * (1.0 - tanh * tanh) * (rate * (1.0 + 3 * 0.044715 * square))
        return (hidden * cdf).astype(BF16), rise

    def predict():
        step = 512
        total = jnp.zeros(out_pred.shape, F32)
        for b in range(up_raw.shape[1] // step):
            hidden = jnp.dot(
                student[...], up_raw[:, b * step : (b + 1) * step], preferred_element_type=F32
            )
            lead = step // (tps * down_raw.shape[2])
            rows_down = down_raw[b * lead : (b + 1) * lead].reshape(step, down_raw.shape[3])
            total = total + jnp.dot(gelu(hidden)[0], rows_down, preferred_element_type=F32)
        out_pred[...] = total

    def share():
        for i, c in enumerate(PROBE):
            keep[c].wait()
            send(("ps", i), xb.at[c], probe_sib.at[i], ps.at[i], pr.at[i], to_sib)

    def activate():
        for c in STUDENT:
            keep[c].wait()

        def rows_of(i, _):
            rows = pl.ds(pl.multiple_of(i * pair, pair), pair)
            hidden = jnp.zeros((pair, up.shape[1]), F32)
            for j, c in enumerate(STUDENT):
                some = xb[c, pl.ds(2 * i, 2)].reshape(pair, feat)
                hidden = hidden + jnp.dot(
                    some, up[j * feat : (j + 1) * feat, :], preferred_element_type=F32
                )
            act[rows, :], slope[rows, :] = gelu(hidden)
            return 0

        lax.fori_loop(0, xn, rows_of, 0)

    steps = dict(
        x0=x0, x1=x1, x2=x2, x3=x3, p=project, k1=k1, k2=k2, k3=k3,
        qs=queries, ks=keys, g=greetings, prep=prepare, act=activate, pred=predict, share=share,
    )
    for step in PLAN:
        steps[step[0]](*step[1:])

    def block_out(k):
        i = lax.rem(x + k, xn)
        for head, (_, total, acc) in enumerate(attend(i, N_X - 1)):
            feats_out[k, :, head] = (acc / total).astype(BF16).reshape(2, chunk, HD)
        if k == 0:
            copy = pltpu.make_async_copy(feats_out.at[k, zh], feats_in.at[tp], local.at[0])
            copy.start()
        else:
            to = along_x(k)
            send(("fa", k), feats_out.at[k, zh], feats_in.at[tp], fs.at[0, k], fr.at[0, k], at_tp(to))
            copy = None
        to = other(along_x(k))
        send(("fb", k), feats_out.at[k, 1 - zh], feats_in.at[tp], fs.at[1, k], fr.at[1, k], at_tp(to))
        return copy

    block_out(1)
    block_out(2)
    block_out(3)
    block_out(0).wait()
    arrived(("ps", 0), ("ps", 1))
    for k in range(xn):
        arrived(("fb", k))
        if k:
            arrived(("fa", k))
    mine = jnp.concatenate([feats_in[p, core] for p in range(tps)], axis=1)
    rest = jnp.concatenate([feats_in[p, 1 - core] for p in range(tps)], axis=1)
    grad_scale = 1.0 / math.sqrt(chunk * tps * toks * grps)

    def diff_of(i):
        target = jnp.dot(
            mine, xb[PROBE[i]].reshape(tps * chunk, feat), preferred_element_type=F32
        ) + jnp.dot(rest, probe_sib[i].reshape(tps * chunk, feat), preferred_element_type=F32)
        diff = out_pred[:, i * feat : (i + 1) * feat] - target
        xb[PRED[i], tp] = (diff * grad_scale).astype(BF16)
        x0(PRED[i])
        return diff

    diff_b = diff_of(1)
    diff_a = diff_of(0)
    squares = jnp.sum((diff_a * diff_a + diff_b * diff_b).reshape(chunk // 8, 8, feat), axis=0)
    loss_tp[tp] = sum(squares[:, i * 128 : (i + 1) * 128] for i in range(feat // 128))
    for d in range(1, tps):
        send(("lt", d), loss_tp.at[tp], loss_tp.at[tp], lt_s.at[d], lt_r.at[d], at_tp(tp_peer(d)))
    x1(PRED[1])
    x1(PRED[0])
    x2(PRED[1])
    x2(PRED[0])
    x3(PRED[1])

    down_mine = down_raw[:, tp].reshape(act.shape[1], 2 * feat)

    def pred(c):
        return xb[c].reshape(tps * chunk, feat)

    def grad_down_of(i):
        acc_down[:, :, :, i * feat : (i + 1) * feat] = lax.dot_general(
            act[...], pred(PRED[i]), (((0,), (0,)), ((), ())), preferred_element_type=F32
        ).reshape(gys, 2, -1, feat)

    def d_act_of(i):
        return lax.dot_general(
            pred(PRED[i]), down_mine[:, i * feat : (i + 1) * feat],
            (((1,), (1,)), ((), ())), preferred_element_type=F32,
        )

    grad_down_of(1)
    d_act = d_act_of(1)
    x3(PRED[0])
    grad_down_of(0)
    for d in range(1, tps):
        arrived(("lt", d))
    loss_core[core] = sum(loss_tp[i] for i in range(tps))
    send("cd", acc_down.at[:, 1 - core], core_down, co_s.at[0], co_r.at[0], to_sib)
    send("cl", loss_core.at[core], loss_core.at[core], co_s.at[1], co_r.at[1], to_sib)
    d_act = d_act + d_act_of(0)
    d_hidden = (d_act * slope[...]).astype(BF16)
    for i, c in enumerate(STUDENT):
        acc_up[i * gys // 2 : (i + 1) * gys // 2] = lax.dot_general(
            xb[c].reshape(tps * chunk, feat), d_hidden,
            (((0,), (0,)), ((), ())), preferred_element_type=F32,
        ).reshape(gys // 2, 2, -1, act.shape[1])
    send("cu", acc_up.at[:, 1 - core], core_up, co_s.at[2], co_r.at[2], to_sib)

    arrived("cd", "cl")
    mine_down[...] = acc_down[:, core] + core_down[...]
    sent_down[...] = mine_down[...].astype(BF16)
    loss_gy[gy] = loss_core[0] + loss_core[1]
    for d in range(1, gys):
        to = gy_peer(d)
        send(("gd", d), sent_down.at[to], got_down.at[d], gy_s.at[0, d], gy_r.at[0, d], at_gy(to))
        send(("gl", d), loss_gy.at[gy], loss_gy.at[gy], gy_s.at[1, d], gy_r.at[1, d], at_gy(to))
    arrived("cu")
    mine_up[...] = acc_up[:, core] + core_up[...]
    sent_up[...] = mine_up[...].astype(BF16)
    for d in range(1, gys):
        to = gy_peer(d)
        send(("gu", d), sent_up.at[to], got_up.at[d], gy_s.at[2, d], gy_r.at[2, d], at_gy(to))
    total = mine_up[gy]
    for d in range(1, gys):
        arrived(("gu", d))
    for d in range(1, gys):
        total = total + got_up[d].astype(F32)
    up_rows[...] = total.reshape(up_rows.shape)
    for d in range(1, tps):
        q = tp_peer(d)
        send(("aa", d), up_rows.at[q], up_got.at[tp], aa_s.at[d], aa_r.at[d], at_tp(q))
    for d in range(1, gys):
        arrived(("gd", d), ("gl", d))
    total = mine_down[gy]
    for d in range(1, gys):
        total = total + got_down[d].astype(F32)
    down_out[...] = total
    loss[...] = sum(loss_gy[i] for i in range(gys))
    up_got[tp] = up_rows[tp]
    for d in range(1, tps):
        arrived(("aa", d))
    up_out[...] = up_got[...]
    for copy in sent.values():
        copy.wait_send()


def on_device(teacher_in, norm_gain, w_qkv, probe, student_in, w_up, w_down):
    grps, toks, tps = sizes = tuple(lax.axis_size(name) for name in ("grp", "tok", "tp"))
    gys, xn = grps * toks // 2, tps // 2
    rows, feat = teacher_in.shape
    depth, _, width = w_qkv.shape
    ff, ds = w_down.shape
    heads, units, chunk = width // HD, ff // tps, rows // N_X
    piece, strip = units // (2 * gys), ds // (2 * gys)
    gain = jnp.broadcast_to(norm_gain.astype(F32)[None, :], (8, feat))
    dma = pltpu.SemaphoreType.DMA
    vmem, hbm = pl.BlockSpec(memory_space=pltpu.VMEM), pl.BlockSpec(memory_space=pl.ANY)
    state = pltpu.VMEM((N_X // 2, heads, 2 * chunk, HD), F32)
    squares, grad_up, grad_down = pl.pallas_call(
        functools.partial(whole_kernel, sizes),
        name="distill",
        out_shape=(
            jax.ShapeDtypeStruct((8, 128), F32),
            jax.ShapeDtypeStruct((tps, strip // tps, units), F32),
            jax.ShapeDtypeStruct((piece, ds), F32),
        ),
        in_specs=[vmem, vmem, hbm, vmem, vmem, hbm, hbm],
        out_specs=[vmem] * 3,
        scratch_shapes=[
            pltpu.VMEM((len(FIRSTS), tps, chunk, feat), BF16),
            pltpu.VMEM((tps, 8, feat), F32),
            pltpu.VMEM((3, depth, width), BF16),
            pltpu.VMEM((chunk, depth), BF16),
            pltpu.VMEM((N_X, chunk, width), BF16),
            pltpu.VMEM((N_X, toks, chunk, 2 * width), BF16),
            state, state, state,
            pltpu.VMEM((ds, ff), BF16),
            pltpu.VMEM((ds, units), BF16),
            pltpu.VMEM((2 * gys, tps, piece, ds), BF16),
            pltpu.VMEM((rows, units), BF16),
            pltpu.VMEM((rows, units), F32),
            pltpu.VMEM((chunk, ds), F32),
            pltpu.VMEM((xn, 2, heads, chunk, HD), BF16),
            pltpu.VMEM((tps, heads, chunk, HD), BF16),
            pltpu.VMEM((2, tps, chunk, feat), BF16),
            pltpu.VMEM((gys, 2, piece, ds), F32),
            pltpu.VMEM((gys, 2, strip, units), F32),
            pltpu.VMEM((gys, piece, ds), F32),
            pltpu.VMEM((gys, strip, units), F32),
            pltpu.VMEM((gys, piece, ds), F32),
            pltpu.VMEM((gys, strip, units), F32),
            pltpu.VMEM((gys, piece, ds), BF16),
            pltpu.VMEM((gys, strip, units), BF16),
            pltpu.VMEM((gys, piece, ds), BF16),
            pltpu.VMEM((gys, strip, units), BF16),
            pltpu.VMEM((tps, strip // tps, units), F32),
            pltpu.VMEM((tps, strip // tps, units), F32),
            pltpu.VMEM((tps, 8, 128), F32),
            pltpu.VMEM((2, 8, 128), F32),
            pltpu.VMEM((gys, 8, 128), F32),
            dma((len(FIRSTS), len(NAMES_X))), dma((len(FIRSTS), len(NAMES_X))),
            dma((tps,)), dma((tps,)),
            dma((N_X, len(NAMES_K))), dma((N_X, len(NAMES_K))),
            dma((3 + PRED[0],)), dma((2, xn)), dma((2, xn)), dma((2,)), dma((2,)),
            dma((tps,)), dma((tps,)), dma((3,)), dma((3,)),
            dma((3, gys)), dma((3, gys)), dma((tps,)), dma((tps,)),
        ],
        compiler_params=pltpu.CompilerParams(
            collective_id=1, has_side_effects=True, vmem_limit_bytes=61 << 20
        ),
    )(
        teacher_in, gain, jnp.transpose(w_qkv, (1, 0, 2)), probe, student_in, w_up,
        w_down.reshape(2 * gys, tps, piece, ds),
    )
    grad_up = grad_up.reshape(tps, -1, 2 * gys, piece).transpose(1, 2, 0, 3).reshape(-1, ff)
    loss = jnp.sum(squares) / (chunk * tps * toks * grps * ds)
    return (loss, grad_up, grad_down)


def solution(mesh):
    placed = (
        P(("grp", "tok"), "tp"),
        P("tp"),
        P(None, None, "tp"),
        P("tp", None),
        P(("grp", "tok", "tp"), None),
        P(),
        P(),
    )
    return jax.shard_map(
        on_device,
        mesh=mesh,
        in_specs=placed,
        out_specs=(P(), P(("grp", "tok", "tp"), None), P(("grp", "tok", "tp"), None)),
        check_vma=False,
    )
```

```python
import functools
import math

import jax
import jax.numpy as jnp
from jax import lax
from jax.experimental import pallas as pl
from jax.experimental.pallas import tpu as pltpu
from jax.sharding import PartitionSpec as P

HD = 128
EXP2_SCALE = math.log2(math.e) / math.sqrt(HD)
MESH = pl.DeviceIdType.MESH
BF16, F32 = jnp.bfloat16, jnp.float32

FIRSTS = ("x", "z") * 4 + ("z",) + ("x", "z") * 2
N_X = 8
PROBE = N_X
STUDENT = (N_X + 1, N_X + 2)
PRED = (N_X + 3, N_X + 4)
NAMES_X = ("z0", "z1", "z2", "z3", "r0", "l0", "r1", "l1", "fr0", "fr1", "fl0", "fl1")
NAMES_K = ("s0", "s1", "s2", "s3", "u0", "d0", "fu", "fd")


def make_plan(early=4):
    n, last = N_X, STUDENT[1]
    plan = [("x0", 0), ("g",)] + [("x0", c) for c in range(1, early)]
    plan += [("prep",), ("x1", 0), ("x1", 1), ("x2", 0), ("pred",)]
    for c in range(n):
        plan += [("x0", c + early)] if c + early <= last else []
        plan += [("x1", c + 2), ("x2", c + 1)]
        if c >= 2:
            plan.append(("k2", c - 2))
        if c >= 3:
            plan.append(("k3", c - 3))
            if c % 2 == 0:
                plan.append(("ks", c // 2 - 1, 0, c - 3))
            plan.append(("qs", 0, c // 2, c - 3))
        if c >= 1:
            plan.append(("k1", c - 1))
        plan += [("x3", c), ("p", c)]
    plan += [("x0", c) for c in range(n + early, last + 1)]
    pair = n // 2 - 1
    plan += [
        ("k2", n - 2), ("ks", pair, 0, 2), ("x3", n), ("k0", n), ("ks", pair, 2, n - 3),
        ("k1", n - 1), ("k3", n - 3), ("qs", 0, n // 2, n - 3), ("k2", n - 1), ("k1", n),
        ("k3", n - 2), ("x2", n + 1), ("x1", n + 2), ("qs", 0, n // 2, n - 2), ("k2", n),
        ("k3", n - 1),
    ]
    return tuple(plan)


PLAN = make_plan()


def whole_kernel(
    sizes, teacher_in, gain, w_hbm, probe, student, up_hbm, down_hbm,
    loss, up_out, down_out,
    xb, gains, w, normed, qb, kvb, top_s, sum_s, acc_s,
    up_raw, up, down_raw, act, slope, out_pred, feats_out, feats_in, shared,
    acc_down, acc_up, core_down, core_up, mine_down, mine_up,
    sent_down, sent_up, got_down, got_up, up_rows, up_got,
    loss_tp, loss_core, loss_gy,
    xs, xr, gs, gr, ks, kr, local, fs, fr,
    lt_s, lt_r, co_s, co_r, gy_s, gy_r, aa_s, aa_r,
):
    grps, toks, tps = sizes
    xn, ys = tps // 2, toks // 2
    gys = grps * ys
    grp, tok, tp = lax.axis_index("grp"), lax.axis_index("tok"), lax.axis_index("tp")
    chunk, feat = xb.shape[2], xb.shape[3]
    half = chunk // 2
    width = qb.shape[2]
    heads = width // HD
    pair = 2 * chunk
    zh, x = lax.rem(tp, 2), tp // 2
    core, y = lax.rem(tok, 2), tok // 2
    gy = grp * ys + y
    zp = tp + 1 - 2 * zh

    def along_x(d):
        return lax.rem(x + d, xn) * 2 + zh

    def along_y(d):
        return lax.rem(y + d, ys) * 2 + core

    def other(slot):
        return slot + 1 - 2 * zh

    def tp_peer(d):
        return lax.rem(tp + d, tps)

    def gy_peer(d):
        return lax.rem(gy + d, gys)

    def at_tp(to):
        return (grp, tok, to)

    def at_gy(to):
        return (to // ys, lax.rem(to, ys) * 2 + core, tp)

    right, left, across = along_x(1), along_x(3), along_x(2)
    above, below, yfar = along_y(1), along_y(3), along_y(2)
    to_z, to_right, to_left = at_tp(zp), at_tp(right), at_tp(left)
    to_up, to_down = (grp, above, tp), (grp, below, tp)
    to_sib = (grp, tok + 1 - 2 * core, tp)

    def room(c, p):
        if c == PROBE:
            return shared.at[tok, p]
        return xb.at[c if c < PROBE else c - 1, p]

    fetch = [
        pltpu.make_async_copy(w_hbm, w, local.at[0]),
        pltpu.make_async_copy(up_hbm, up_raw, local.at[1]),
        pltpu.make_async_copy(down_hbm, down_raw, local.at[2]),
    ]
    keep = [
        pltpu.make_async_copy(
            teacher_in.at[pl.ds(c * chunk, chunk), :], xb.at[c, tp], local.at[3 + c]
        )
        for c in range(N_X)
    ] + [
        pltpu.make_async_copy(
            student.at[:, pl.ds(i * feat, feat)], room(c, tp), local.at[3 + N_X + i]
        )
        for i, c in enumerate(STUDENT)
    ]
    for copy in keep + fetch:
        copy.start()
    gains[tp] = gain[...]
    piece_rows = shared.shape[2] // 2
    probe_rows = pl.ds(pl.multiple_of(tok * piece_rows, piece_rows), piece_rows)
    for i in range(2):
        shared[tok, tp, i * piece_rows : (i + 1) * piece_rows, :] = probe[
            probe_rows, i * feat : (i + 1) * feat
        ]

    barrier = pltpu.get_barrier_semaphore()
    greet = [at_tp(tp_peer(d)) for d in range(1, tps)]
    greet += [at_gy(gy_peer(d)) for d in range(1, gys)] + [to_sib]
    for device in greet:
        pl.semaphore_signal(barrier, inc=1, device_id=device, device_id_type=MESH)
    pl.semaphore_wait(barrier, len(greet))

    sent = {}

    def send(name, src, dst, ssem, rsem, device):
        copy = pltpu.make_async_remote_copy(
            src_ref=src, dst_ref=dst, send_sem=ssem, recv_sem=rsem,
            device_id=device, device_id_type=MESH,
        )
        copy.start()
        sent[name] = copy

    def arrived(*names):
        for name in names:
            sent[name].wait_recv()


    def send_x(name, c, ref, device):
        i = NAMES_X.index(name)
        send((name, c), ref[0], ref[1], xs.at[c, i], xr.at[c, i], device)

    def own(c):
        to = room(c, tp)
        if c < N_X:
            return teacher_in.at[pl.ds(c * chunk, chunk), :], to
        if c in STUDENT:
            return student.at[:, pl.ds(STUDENT.index(c) * feat, feat)], to
        return to, to

    def slot(c, p):
        return room(c, p), room(c, p)

    def part(c, p, h):
        rows = (2 * piece_rows if c == PROBE else chunk) // 2
        ref = room(c, p).at[pl.ds(h * rows, rows), :]
        return ref, ref

    def x0(c):
        if FIRSTS[c] == "z":
            send_x("z0", c, own(c), to_z)
        send_x("r0", c, own(c), to_right)
        send_x("l0", c, own(c), to_left)
        if FIRSTS[c] == "x":
            send_x("z0", c, own(c), to_z)

    def x1(c):
        if FIRSTS[c] == "z":
            arrived(("z0", c))
            send_x("r1", c, slot(c, zp), to_right)
            send_x("l1", c, slot(c, zp), to_left)
        else:
            arrived(("r0", c))
            send_x("fr0", c, part(c, left, 0), to_right)
            send_x("z1", c, slot(c, left), to_z)
            arrived(("l0", c))
            send_x("fl0", c, part(c, right, 1), to_left)
            send_x("z2", c, slot(c, right), to_z)

    def x2(c):
        if FIRSTS[c] == "z":
            arrived(("r0", c))
            send_x("fr0", c, part(c, left, 0), to_right)
            arrived(("l0", c))
            send_x("fl0", c, part(c, right, 1), to_left)
            arrived(("r1", c))
            send_x("fr1", c, part(c, other(left), 0), to_right)
            arrived(("l1", c))
            send_x("fl1", c, part(c, other(right), 1), to_left)
        else:
            arrived(("fr0", c), ("fl0", c))
            send_x("z3", c, slot(c, across), to_z)

    def x3(c):
        if FIRSTS[c] == "z":
            arrived(("fr0", c), ("fl0", c), ("fr1", c), ("fl1", c))
        else:
            arrived(("z0", c), ("z1", c), ("z2", c), ("z3", c))

    def greetings():
        for d in range(1, tps):
            send(("g", d), gains.at[tp], gains.at[tp], gs.at[d], gr.at[d], at_tp(tp_peer(d)))
        top_s[...] = jnp.full(top_s.shape, -1e30, F32)
        sum_s[...] = jnp.zeros(sum_s.shape, F32)
        acc_s[...] = jnp.zeros(acc_s.shape, F32)

    def prepare():
        fetch[1].wait()
        ff, units = up_raw.shape[1], up.shape[1]
        piece = units // (2 * gys)
        step = 512
        total = jnp.zeros(up.shape, F32)
        for b in range(ff // step):
            row = lax.broadcasted_iota(jnp.int32, (step, units), 0) + b * step
            col = lax.broadcasted_iota(jnp.int32, (step, units), 1)
            rest = jnp.bitwise_and(col, piece - 1)
            unit = (col - rest) * tps + tp * piece + rest
            pick = jnp.where(row == unit, 1.0, 0.0).astype(BF16)
            total = total + jnp.dot(
                up_raw[:, b * step : (b + 1) * step], pick, preferred_element_type=F32
            )
        up[...] = total.astype(BF16)
        fetch[0].wait()
        fetch[2].wait()
        for d in range(1, tps):
            arrived(("g", d))


    def send_k(name, c, ref, device):
        i = NAMES_K.index(name)
        send((name, c), ref, ref, ks.at[c, i], kr.at[c, i], device)

    def project(c):
        keep[c].wait()
        step = 64

        def rows_of(i, _):
            rows = pl.ds(pl.multiple_of(i * step, step), step)
            squares = jnp.zeros((step, feat), F32)
            for p in range(tps):
                some = xb[c, p, rows, :].astype(F32)
                squares = squares + some * some
            mean = jnp.sum(squares, axis=1, keepdims=True) / (tps * feat)
            scale = lax.rsqrt(mean + 1e-05)
            for p in range(tps):
                some = xb[c, p, rows, :].astype(F32)
                normed[rows, p * feat : (p + 1) * feat] = (
                    some * scale * gains[p, 0:1, :]
                ).astype(BF16)
            return 0

        lax.fori_loop(0, chunk // step, rows_of, 0)
        for j in (1, 2):
            kvb[c, tok, :, (j - 1) * width : j * width] = jnp.dot(
                normed[...], w[j], preferred_element_type=F32
            ).astype(BF16)
        k0(c)
        qb[c] = jnp.dot(normed[...], w[0], preferred_element_type=F32).astype(BF16)

    def place(c, t):
        return shared.at[t] if c == PROBE else kvb.at[c, t]

    def place_half(c, t, h):
        if c == PROBE:
            return shared.at[t, pl.ds(h * tps // 2, tps // 2)]
        return kvb.at[c, t, pl.ds(h * half, half), :]

    def k0(c):
        send_k("u0", c, place(c, tok), to_up)
        send_k("d0", c, place(c, tok), to_down)
        send_k("s0", c, place(c, tok), to_sib)

    def k1(c):
        arrived(("u0", c))
        send_k("fu", c, place_half(c, below, 0), to_up)
        send_k("s1", c, place(c, below), to_sib)
        arrived(("d0", c))
        send_k("fd", c, place_half(c, above, 1), to_down)
        send_k("s2", c, place(c, above), to_sib)

    def k2(c):
        arrived(("fu", c), ("fd", c))
        send_k("s3", c, place(c, yfar), to_sib)

    def k3(c):
        arrived(("s0", c), ("s1", c), ("s2", c), ("s3", c))

    def attend(i, c):
        result = []
        for head in range(heads):
            cols = slice(head * HD, (head + 1) * HD)
            vcols = slice(width + head * HD, width + (head + 1) * HD)
            query = qb[pl.ds(2 * i, 2), :, cols].reshape(pair, HD)
            top = top_s[i, head][:, :1]
            keys = kvb[c, :, :, cols].reshape(toks * chunk, HD)
            values = kvb[c, :, :, vcols].reshape(toks * chunk, HD)
            scores = lax.dot_general(
                query, keys, (((1,), (1,)), ((), ())), preferred_element_type=F32
            )
            top_new = jnp.maximum(top, jnp.max(scores, axis=1, keepdims=True))
            fade = jnp.exp2((top - top_new) * EXP2_SCALE)
            weights = jnp.exp2(scores * EXP2_SCALE - top_new * EXP2_SCALE).astype(BF16)
            both = jnp.concatenate([values, jnp.ones_like(values)], axis=1)
            res = jnp.dot(weights, both, preferred_element_type=F32)
            result.append(
                (top_new, sum_s[i, head] * fade + res[:, HD:], acc_s[i, head] * fade + res[:, :HD])
            )
        return result

    def attend_keep(i, c):
        for head, (top, total, acc) in enumerate(attend(i, c)):
            top_s[i, head] = jnp.broadcast_to(top, (pair, HD))
            sum_s[i, head] = total
            acc_s[i, head] = acc
        return 0

    def queries(lo, hi, c):
        lax.fori_loop(lo, hi, lambda i, _: attend_keep(i, c), 0)

    def keys(i, lo, hi):
        lax.fori_loop(lo, hi, lambda c, _: attend_keep(i, c), 0)

    def gelu(hidden):
        rate = math.sqrt(2 / math.pi)
        square = hidden * hidden
        tanh = jnp.tanh(rate * (hidden + 0.044715 * (hidden * square)))
        cdf = 0.5 * (1.0 + tanh)
        rise = cdf + 0.5 * hidden * (1.0 - tanh * tanh) * (rate * (1.0 + 3 * 0.044715 * square))
        return (hidden * cdf).astype(BF16), rise

    def predict():
        step = 512
        total = jnp.zeros(out_pred.shape, F32)
        for b in range(up_raw.shape[1] // step):
            hidden = jnp.dot(
                student[...], up_raw[:, b * step : (b + 1) * step], preferred_element_type=F32
            )
            lead = step // (tps * down_raw.shape[2])
            rows_down = down_raw[b * lead : (b + 1) * lead].reshape(step, down_raw.shape[3])
            total = total + jnp.dot(gelu(hidden)[0], rows_down, preferred_element_type=F32)
        out_pred[...] = total

    def activate():
        for copy in keep[N_X:]:
            copy.wait()

        def rows_of(i, _):
            rows = pl.ds(pl.multiple_of(i * pair, pair), pair)
            hidden = jnp.zeros((pair, up.shape[1]), F32)
            for j, c in enumerate(STUDENT):
                some = xb[c - 1, pl.ds(2 * i, 2)].reshape(pair, feat)
                hidden = hidden + jnp.dot(
                    some, up[j * feat : (j + 1) * feat, :], preferred_element_type=F32
                )
            act[rows, :], slope[rows, :] = gelu(hidden)
            return 0

        lax.fori_loop(0, xn, rows_of, 0)

    steps = dict(
        x0=x0, x1=x1, x2=x2, x3=x3, p=project, k0=k0, k1=k1, k2=k2, k3=k3,
        qs=queries, ks=keys, g=greetings, prep=prepare, pred=predict,
    )
    for step in PLAN:
        steps[step[0]](*step[1:])

    def block_out(k):
        i = lax.rem(x + k, xn)
        for head, (_, total, acc) in enumerate(attend(i, N_X - 1)):
            feats_out[k, :, head] = (acc / total).astype(BF16).reshape(2, chunk, HD)
        if k == 0:
            copy = pltpu.make_async_copy(feats_out.at[k, zh], feats_in.at[tp], local.at[0])
            copy.start()
        else:
            to = along_x(k)
            send(("fa", k), feats_out.at[k, zh], feats_in.at[tp], fs.at[0, k], fr.at[0, k], at_tp(to))
            copy = None
        to = other(along_x(k))
        send(("fb", k), feats_out.at[k, 1 - zh], feats_in.at[tp], fs.at[1, k], fr.at[1, k], at_tp(to))
        return copy

    block_out(1)
    block_out(2)
    x2(STUDENT[1])
    block_out(3)
    block_out(0).wait()
    k3(PROBE)
    for k in range(xn):
        arrived(("fb", k))
        if k:
            arrived(("fa", k))
    grad_scale = 1.0 / math.sqrt(chunk * tps * toks * grps)

    def diff_of(i):
        target = jnp.zeros((chunk, feat), F32)
        for p in range(tps):
            feats = jnp.concatenate([feats_in[p, head] for head in range(heads)], axis=1)
            block = shared[:, p, i * piece_rows : (i + 1) * piece_rows, :].reshape(width, feat)
            target = target + jnp.dot(feats, block, preferred_element_type=F32)
        diff = out_pred[:, i * feat : (i + 1) * feat] - target
        xb[PRED[i] - 1, tp] = (diff * grad_scale).astype(BF16)
        x0(PRED[i])
        return diff

    diff_b = diff_of(1)
    diff_a = diff_of(0)
    squares = jnp.sum((diff_a * diff_a + diff_b * diff_b).reshape(chunk // 8, 8, feat), axis=0)
    loss_tp[tp] = sum(squares[:, i * 128 : (i + 1) * 128] for i in range(feat // 128))
    for d in range(1, tps):
        send(("lt", d), loss_tp.at[tp], loss_tp.at[tp], lt_s.at[d], lt_r.at[d], at_tp(tp_peer(d)))
    x3(STUDENT[0])
    x3(STUDENT[1])
    x1(PRED[1])
    x1(PRED[0])
    activate()
    x2(PRED[1])
    x2(PRED[0])
    x3(PRED[1])

    down_mine = down_raw[:, tp].reshape(act.shape[1], 2 * feat)

    def pred(c):
        return xb[c - 1].reshape(tps * chunk, feat)

    def grad_down_of(i):
        acc_down[:, :, :, i * feat : (i + 1) * feat] = lax.dot_general(
            act[...], pred(PRED[i]), (((0,), (0,)), ((), ())), preferred_element_type=F32
        ).reshape(gys, 2, -1, feat)

    def d_act_of(i):
        return lax.dot_general(
            pred(PRED[i]), down_mine[:, i * feat : (i + 1) * feat],
            (((1,), (1,)), ((), ())), preferred_element_type=F32,
        )

    d_act = d_act_of(1)
    grad_down_of(1)
    x3(PRED[0])
    d_hidden = ((d_act + d_act_of(0)) * slope[...]).astype(BF16)
    for i, c in enumerate(STUDENT):
        acc_up[i * gys // 2 : (i + 1) * gys // 2] = lax.dot_general(
            pred(c), d_hidden, (((0,), (0,)), ((), ())), preferred_element_type=F32,
        ).reshape(gys // 2, 2, -1, act.shape[1])
    send("cu", acc_up.at[:, 1 - core], core_up, co_s.at[2], co_r.at[2], to_sib)
    grad_down_of(0)
    send("cd", acc_down.at[:, 1 - core], core_down, co_s.at[0], co_r.at[0], to_sib)
    for d in range(1, tps):
        arrived(("lt", d))
    loss_core[core] = sum(loss_tp[i] for i in range(tps))
    send("cl", loss_core.at[core], loss_core.at[core], co_s.at[1], co_r.at[1], to_sib)

    arrived("cu")
    mine_up[...] = acc_up[:, core] + core_up[...]
    sent_up[...] = mine_up[...].astype(BF16)
    for d in range(1, gys):
        to = gy_peer(d)
        send(("gu", d), sent_up.at[to], got_up.at[d], gy_s.at[2, d], gy_r.at[2, d], at_gy(to))
    arrived("cd", "cl")
    mine_down[...] = acc_down[:, core] + core_down[...]
    sent_down[...] = mine_down[...].astype(BF16)
    loss_gy[gy] = loss_core[0] + loss_core[1]
    for d in range(1, gys):
        to = gy_peer(d)
        send(("gd", d), sent_down.at[to], got_down.at[d], gy_s.at[0, d], gy_r.at[0, d], at_gy(to))
        send(("gl", d), loss_gy.at[gy], loss_gy.at[gy], gy_s.at[1, d], gy_r.at[1, d], at_gy(to))
    total = mine_up[gy]
    for d in range(1, gys):
        arrived(("gu", d))
    for d in range(1, gys):
        total = total + got_up[d].astype(F32)
    up_rows[...] = total.reshape(up_rows.shape)
    for d in range(1, tps):
        q = tp_peer(d)
        send(("aa", d), up_rows.at[q], up_got.at[tp], aa_s.at[d], aa_r.at[d], at_tp(q))
    for d in range(1, gys):
        arrived(("gd", d), ("gl", d))
    total = mine_down[gy]
    for d in range(1, gys):
        total = total + got_down[d].astype(F32)
    down_out[...] = total
    loss[...] = sum(loss_gy[i] for i in range(gys))
    up_got[tp] = up_rows[tp]
    for d in range(1, tps):
        arrived(("aa", d))
    up_out[...] = up_got[...]
    for copy in sent.values():
        copy.wait_send()


def on_device(teacher_in, norm_gain, w_qkv, probe, student_in, w_up, w_down):
    grps, toks, tps = sizes = tuple(lax.axis_size(name) for name in ("grp", "tok", "tp"))
    gys, xn = grps * toks // 2, tps // 2
    rows, feat = teacher_in.shape
    depth, _, width = w_qkv.shape
    ff, ds = w_down.shape
    heads, units, chunk = width // HD, ff // tps, rows // N_X
    piece, strip = units // (2 * gys), ds // (2 * gys)
    gain = jnp.broadcast_to(norm_gain.astype(F32)[None, :], (8, feat))
    dma = pltpu.SemaphoreType.DMA
    vmem, hbm = pl.BlockSpec(memory_space=pltpu.VMEM), pl.BlockSpec(memory_space=pl.ANY)
    state = pltpu.VMEM((N_X // 2, heads, 2 * chunk, HD), F32)
    squares, grad_up, grad_down = pl.pallas_call(
        functools.partial(whole_kernel, sizes),
        name="distill",
        out_shape=(
            jax.ShapeDtypeStruct((8, 128), F32),
            jax.ShapeDtypeStruct((tps, strip // tps, units), F32),
            jax.ShapeDtypeStruct((piece, ds), F32),
        ),
        in_specs=[vmem, vmem, hbm, vmem, vmem, hbm, hbm],
        out_specs=[vmem] * 3,
        scratch_shapes=[
            pltpu.VMEM((len(FIRSTS) - 1, tps, chunk, feat), BF16),
            pltpu.VMEM((tps, 8, feat), F32),
            pltpu.VMEM((3, depth, width), BF16),
            pltpu.VMEM((chunk, depth), BF16),
            pltpu.VMEM((N_X, chunk, width), BF16),
            pltpu.VMEM((N_X, toks, chunk, 2 * width), BF16),
            state, state, state,
            pltpu.VMEM((ds, ff), BF16),
            pltpu.VMEM((ds, units), BF16),
            pltpu.VMEM((2 * gys, tps, piece, ds), BF16),
            pltpu.VMEM((rows, units), BF16),
            pltpu.VMEM((rows, units), F32),
            pltpu.VMEM((chunk, ds), F32),
            pltpu.VMEM((xn, 2, heads, chunk, HD), BF16),
            pltpu.VMEM((tps, heads, chunk, HD), BF16),
            pltpu.VMEM((toks, tps, 2 * width // toks, feat), BF16),
            pltpu.VMEM((gys, 2, piece, ds), F32),
            pltpu.VMEM((gys, 2, strip, units), F32),
            pltpu.VMEM((gys, piece, ds), F32),
            pltpu.VMEM((gys, strip, units), F32),
            pltpu.VMEM((gys, piece, ds), F32),
            pltpu.VMEM((gys, strip, units), F32),
            pltpu.VMEM((gys, piece, ds), BF16),
            pltpu.VMEM((gys, strip, units), BF16),
            pltpu.VMEM((gys, piece, ds), BF16),
            pltpu.VMEM((gys, strip, units), BF16),
            pltpu.VMEM((tps, strip // tps, units), F32),
            pltpu.VMEM((tps, strip // tps, units), F32),
            pltpu.VMEM((tps, 8, 128), F32),
            pltpu.VMEM((2, 8, 128), F32),
            pltpu.VMEM((gys, 8, 128), F32),
            dma((len(FIRSTS), len(NAMES_X))), dma((len(FIRSTS), len(NAMES_X))),
            dma((tps,)), dma((tps,)),
            dma((N_X + 1, len(NAMES_K))), dma((N_X + 1, len(NAMES_K))),
            dma((5 + N_X,)), dma((2, xn)), dma((2, xn)),
            dma((tps,)), dma((tps,)), dma((3,)), dma((3,)),
            dma((3, gys)), dma((3, gys)), dma((tps,)), dma((tps,)),
        ],
        compiler_params=pltpu.CompilerParams(
            collective_id=1, has_side_effects=True, vmem_limit_bytes=61 << 20
        ),
    )(
        teacher_in, gain, jnp.transpose(w_qkv, (1, 0, 2)), probe, student_in, w_up,
        w_down.reshape(2 * gys, tps, piece, ds),
    )
    grad_up = grad_up.reshape(tps, -1, 2 * gys, piece).transpose(1, 2, 0, 3).reshape(-1, ff)
    loss = jnp.sum(squares) / (chunk * tps * toks * grps * ds)
    return (loss, grad_up, grad_down)


def solution(mesh):
    placed = (
        P(("grp", "tok"), "tp"),
        P("tp"),
        P(None, None, "tp"),
        P("tp", None),
        P(("grp", "tok", "tp"), None),
        P(),
        P(),
    )
    return jax.shard_map(
        on_device,
        mesh=mesh,
        in_specs=placed,
        out_specs=(P(), P(("grp", "tok", "tp"), None), P(("grp", "tok", "tp"), None)),
        check_vma=False,
    )
```

```python
import functools
import math

import jax
import jax.numpy as jnp
from jax import lax
from jax.experimental import pallas as pl
from jax.experimental.pallas import tpu as pltpu
from jax.sharding import PartitionSpec as P

HD = 128
EXP2_SCALE = math.log2(math.e) / math.sqrt(HD)
MESH = pl.DeviceIdType.MESH
BF16, F32 = jnp.bfloat16, jnp.float32

FIRSTS = ("x", "z") * 4 + ("z",) + ("x", "z") * 2
N_X = 8
PROBE = N_X
STUDENT = (N_X + 1, N_X + 2)
PRED = (N_X + 3, N_X + 4)
NAMES_X = ("z0", "z1", "z2", "z3", "r0", "l0", "r1", "l1", "fr0", "fr1", "fl0", "fl1")
NAMES_K = ("s0", "s1", "s2", "s3", "u0", "d0", "fu", "fd")


def make_plan(early=6, first=4, second=2):
    n, last = N_X, STUDENT[1]
    plan = [("x0", 0), ("g",)] + [("x0", c) for c in range(1, early)]
    plan.append(("prep",))
    plan += [("x1", c) for c in range(first)] + [("x2", c) for c in range(second)] + [("pred",)]
    for c in range(n):
        plan += [("x0", c + early)] if c + early <= last else []
        plan += [("x1", c + first)] if c + first <= last else []
        plan.append(("x2", c + second))
        if c >= 2:
            plan.append(("k2", c - 2))
        if c >= 3:
            plan.append(("k3", c - 3))
            if c % 2 == 0:
                plan.append(("ks", c // 2 - 1, 0, c - 3))
            plan.append(("qs", 0, c // 2, c - 3))
        if c >= 1:
            plan.append(("k1", c - 1))
        plan += [("x3", c), ("p", c)]
    late = [("x1", c) for c in range(n + first, last + 1)]
    late += [("x2", c) for c in range(n + second, last)]
    pair = n // 2 - 1
    plan += [
        ("k2", n - 2), ("ks", pair, 0, 2), ("x3", n), ("k0", n), ("ks", pair, 2, n - 3),
        ("k1", n - 1), ("k3", n - 3), ("qs", 0, n // 2, n - 3), ("k2", n - 1), ("k1", n),
        ("k3", n - 2), *late, ("qs", 0, n // 2, n - 2), ("k2", n),
        ("k3", n - 1),
    ]
    return tuple(plan)


PLAN = make_plan()


def whole_kernel(
    sizes, teacher_in, gain, w_hbm, probe, student, up_hbm, down_hbm,
    loss, up_out, down_out,
    xb, gains, w, normed, qb, kvb, top_s, sum_s, acc_s,
    up_raw, up, down_raw, act, slope, out_pred, feats_out, feats_in, shared,
    acc_down, acc_up, core_down, core_up, mine_down, mine_up,
    sent_down, sent_up, got_down, got_up, up_rows, up_got,
    loss_tp, loss_core, loss_gy,
    xs, xr, gs, gr, ks, kr, local, fs, fr,
    lt_s, lt_r, co_s, co_r, gy_s, gy_r, aa_s, aa_r,
):
    grps, toks, tps = sizes
    xn, ys = tps // 2, toks // 2
    gys = grps * ys
    grp, tok, tp = lax.axis_index("grp"), lax.axis_index("tok"), lax.axis_index("tp")
    chunk, feat = xb.shape[2], xb.shape[3]
    half = chunk // 2
    width = qb.shape[2]
    heads = width // HD
    pair = 2 * chunk
    zh, x = lax.rem(tp, 2), tp // 2
    core, y = lax.rem(tok, 2), tok // 2
    gy = grp * ys + y
    zp = tp + 1 - 2 * zh

    def along_x(d):
        return lax.rem(x + d, xn) * 2 + zh

    def along_y(d):
        return lax.rem(y + d, ys) * 2 + core

    def other(slot):
        return slot + 1 - 2 * zh

    def tp_peer(d):
        return lax.rem(tp + d, tps)

    def gy_peer(d):
        return lax.rem(gy + d, gys)

    def at_tp(to):
        return (grp, tok, to)

    def at_gy(to):
        return (to // ys, lax.rem(to, ys) * 2 + core, tp)

    right, left, across = along_x(1), along_x(3), along_x(2)
    above, below, yfar = along_y(1), along_y(3), along_y(2)
    to_z, to_right, to_left = at_tp(zp), at_tp(right), at_tp(left)
    to_up, to_down = (grp, above, tp), (grp, below, tp)
    to_sib = (grp, tok + 1 - 2 * core, tp)

    def room(c, p):
        if c == PROBE:
            return shared.at[tok, p]
        return xb.at[c if c < PROBE else c - 1, p]

    fetch = [
        pltpu.make_async_copy(w_hbm, w, local.at[0]),
        pltpu.make_async_copy(up_hbm, up_raw, local.at[1]),
        pltpu.make_async_copy(down_hbm, down_raw, local.at[2]),
    ]
    keep = [
        pltpu.make_async_copy(
            teacher_in.at[pl.ds(c * chunk, chunk), :], xb.at[c, tp], local.at[3 + c]
        )
        for c in range(N_X)
    ] + [
        pltpu.make_async_copy(
            student.at[:, pl.ds(i * feat, feat)], room(c, tp), local.at[3 + N_X + i]
        )
        for i, c in enumerate(STUDENT)
    ]
    for copy in keep + fetch:
        copy.start()
    gains[tp] = gain[...]
    piece_rows = shared.shape[2] // 2
    probe_rows = pl.ds(pl.multiple_of(tok * piece_rows, piece_rows), piece_rows)
    for i in range(2):
        shared[tok, tp, i * piece_rows : (i + 1) * piece_rows, :] = probe[
            probe_rows, i * feat : (i + 1) * feat
        ]

    barrier = pltpu.get_barrier_semaphore()
    greet = [at_tp(tp_peer(d)) for d in range(1, tps)]
    greet += [at_gy(gy_peer(d)) for d in range(1, gys)] + [to_sib]
    for device in greet:
        pl.semaphore_signal(barrier, inc=1, device_id=device, device_id_type=MESH)
    pl.semaphore_wait(barrier, len(greet))

    sent = {}

    def send(name, src, dst, ssem, rsem, device):
        copy = pltpu.make_async_remote_copy(
            src_ref=src, dst_ref=dst, send_sem=ssem, recv_sem=rsem,
            device_id=device, device_id_type=MESH,
        )
        copy.start()
        sent[name] = copy

    def arrived(*names):
        for name in names:
            sent[name].wait_recv()


    def send_x(name, c, ref, device):
        i = NAMES_X.index(name)
        send((name, c), ref[0], ref[1], xs.at[c, i], xr.at[c, i], device)

    def own(c):
        to = room(c, tp)
        if c < N_X:
            return teacher_in.at[pl.ds(c * chunk, chunk), :], to
        if c in STUDENT:
            return student.at[:, pl.ds(STUDENT.index(c) * feat, feat)], to
        return to, to

    def slot(c, p):
        return room(c, p), room(c, p)

    def part(c, p, h):
        rows = (2 * piece_rows if c == PROBE else chunk) // 2
        ref = room(c, p).at[pl.ds(h * rows, rows), :]
        return ref, ref

    def x0(c):
        if FIRSTS[c] == "z":
            send_x("z0", c, own(c), to_z)
        send_x("r0", c, own(c), to_right)
        send_x("l0", c, own(c), to_left)
        if FIRSTS[c] == "x":
            send_x("z0", c, own(c), to_z)

    def x1(c):
        if FIRSTS[c] == "z":
            arrived(("z0", c))
            send_x("r1", c, slot(c, zp), to_right)
            send_x("l1", c, slot(c, zp), to_left)
        else:
            arrived(("r0", c))
            send_x("fr0", c, part(c, left, 0), to_right)
            send_x("z1", c, slot(c, left), to_z)
            arrived(("l0", c))
            send_x("fl0", c, part(c, right, 1), to_left)
            send_x("z2", c, slot(c, right), to_z)

    def x2(c):
        if FIRSTS[c] == "z":
            arrived(("r0", c))
            send_x("fr0", c, part(c, left, 0), to_right)
            arrived(("l0", c))
            send_x("fl0", c, part(c, right, 1), to_left)
            arrived(("r1", c))
            send_x("fr1", c, part(c, other(left), 0), to_right)
            arrived(("l1", c))
            send_x("fl1", c, part(c, other(right), 1), to_left)
        else:
            arrived(("fr0", c), ("fl0", c))
            send_x("z3", c, slot(c, across), to_z)

    def x3(c):
        if FIRSTS[c] == "z":
            arrived(("fr0", c), ("fl0", c), ("fr1", c), ("fl1", c))
        else:
            arrived(("z0", c), ("z1", c), ("z2", c), ("z3", c))

    def greetings():
        for d in range(1, tps):
            send(("g", d), gains.at[tp], gains.at[tp], gs.at[d], gr.at[d], at_tp(tp_peer(d)))
        top_s[...] = jnp.full(top_s.shape, -1e30, F32)
        sum_s[...] = jnp.zeros(sum_s.shape, F32)
        acc_s[...] = jnp.zeros(acc_s.shape, F32)

    def prepare():
        fetch[1].wait()
        ff, units = up_raw.shape[1], up.shape[1]
        piece = units // (2 * gys)
        step = 512

        def add(b, total):
            row = lax.broadcasted_iota(jnp.int32, (step, units), 0) + b * step
            col = lax.broadcasted_iota(jnp.int32, (step, units), 1)
            rest = jnp.bitwise_and(col, piece - 1)
            unit = (col - rest) * tps + tp * piece + rest
            pick = jnp.where(row == unit, 1.0, 0.0).astype(BF16)
            cols = pl.ds(pl.multiple_of(b * step, step), step)
            return total + jnp.dot(up_raw[:, cols], pick, preferred_element_type=F32)

        up[...] = lax.fori_loop(0, ff // step, add, jnp.zeros(up.shape, F32)).astype(BF16)
        fetch[0].wait()
        fetch[2].wait()
        for d in range(1, tps):
            arrived(("g", d))


    def send_k(name, c, ref, device):
        i = NAMES_K.index(name)
        send((name, c), ref, ref, ks.at[c, i], kr.at[c, i], device)

    def project(c):
        keep[c].wait()
        step = 64

        def rows_of(i, _):
            rows = pl.ds(pl.multiple_of(i * step, step), step)
            squares = jnp.zeros((step, feat), F32)
            for p in range(tps):
                some = xb[c, p, rows, :].astype(F32)
                squares = squares + some * some
            mean = jnp.sum(squares, axis=1, keepdims=True) / (tps * feat)
            scale = lax.rsqrt(mean + 1e-05)
            for p in range(tps):
                some = xb[c, p, rows, :].astype(F32)
                normed[rows, p * feat : (p + 1) * feat] = (
                    some * scale * gains[p, 0:1, :]
                ).astype(BF16)
            return 0

        lax.fori_loop(0, chunk // step, rows_of, 0)

        def key_value(j, _):
            cols = pl.ds(pl.multiple_of(j * width, width), width)
            kvb[c, tok, :, cols] = jnp.dot(
                normed[...], w[j + 1], preferred_element_type=F32
            ).astype(BF16)
            return 0

        lax.fori_loop(0, 2, key_value, 0)
        k0(c)
        qb[c] = jnp.dot(normed[...], w[0], preferred_element_type=F32).astype(BF16)

    def place(c, t):
        return shared.at[t] if c == PROBE else kvb.at[c, t]

    def place_half(c, t, h):
        if c == PROBE:
            return shared.at[t, pl.ds(h * tps // 2, tps // 2)]
        return kvb.at[c, t, pl.ds(h * half, half), :]

    def k0(c):
        send_k("u0", c, place(c, tok), to_up)
        send_k("d0", c, place(c, tok), to_down)
        send_k("s0", c, place(c, tok), to_sib)

    def k1(c):
        arrived(("u0", c))
        send_k("fu", c, place_half(c, below, 0), to_up)
        send_k("s1", c, place(c, below), to_sib)
        arrived(("d0", c))
        send_k("fd", c, place_half(c, above, 1), to_down)
        send_k("s2", c, place(c, above), to_sib)

    def k2(c):
        arrived(("fu", c), ("fd", c))
        send_k("s3", c, place(c, yfar), to_sib)

    def k3(c):
        arrived(("s0", c), ("s1", c), ("s2", c), ("s3", c))

    def attend(i, c):
        result = []
        for head in range(heads):
            cols = slice(head * HD, (head + 1) * HD)
            vcols = slice(width + head * HD, width + (head + 1) * HD)
            query = qb[pl.ds(2 * i, 2), :, cols].reshape(pair, HD)
            top = top_s[i, head][:, :1]
            keys = kvb[c, :, :, cols].reshape(toks * chunk, HD)
            values = kvb[c, :, :, vcols].reshape(toks * chunk, HD)
            scores = lax.dot_general(
                query, keys, (((1,), (1,)), ((), ())), preferred_element_type=F32
            )
            top_new = jnp.maximum(top, jnp.max(scores, axis=1, keepdims=True))
            fade = jnp.exp2((top - top_new) * EXP2_SCALE)
            weights = jnp.exp2(scores * EXP2_SCALE - top_new * EXP2_SCALE).astype(BF16)
            both = jnp.concatenate([values, jnp.ones_like(values)], axis=1)
            res = jnp.dot(weights, both, preferred_element_type=F32)
            result.append(
                (top_new, sum_s[i, head] * fade + res[:, HD:], acc_s[i, head] * fade + res[:, :HD])
            )
        return result

    def attend_keep(i, c):
        for head, (top, total, acc) in enumerate(attend(i, c)):
            top_s[i, head] = jnp.broadcast_to(top, (pair, HD))
            sum_s[i, head] = total
            acc_s[i, head] = acc
        return 0

    def queries(lo, hi, c):
        lax.fori_loop(lo, hi, lambda i, _: attend_keep(i, c), 0)

    def keys(i, lo, hi):
        lax.fori_loop(lo, hi, lambda c, _: attend_keep(i, c), 0)

    def gelu(hidden):
        rate = math.sqrt(2 / math.pi)
        square = hidden * hidden
        tanh = jnp.tanh(rate * (hidden + 0.044715 * (hidden * square)))
        cdf = 0.5 * (1.0 + tanh)
        rise = cdf + 0.5 * hidden * (1.0 - tanh * tanh) * (rate * (1.0 + 3 * 0.044715 * square))
        return (hidden * cdf).astype(BF16), rise

    def predict():
        step = 512
        out_pred[...] = jnp.zeros(out_pred.shape, F32)
        lead = step // (tps * down_raw.shape[2])

        def add(b, _):
            cols = pl.ds(pl.multiple_of(b * step, step), step)
            hidden = jnp.dot(student[...], up_raw[:, cols], preferred_element_type=F32)
            rows_down = down_raw[pl.ds(b * lead, lead)].reshape(step, down_raw.shape[3])
            out_pred[...] += jnp.dot(gelu(hidden)[0], rows_down, preferred_element_type=F32)
            return 0

        lax.fori_loop(0, up_raw.shape[1] // step, add, 0)

    def activate():
        for copy in keep[N_X:]:
            copy.wait()

        def rows_of(i, _):
            rows = pl.ds(pl.multiple_of(i * pair, pair), pair)
            hidden = jnp.zeros((pair, up.shape[1]), F32)
            for j, c in enumerate(STUDENT):
                some = xb[c - 1, pl.ds(2 * i, 2)].reshape(pair, feat)
                hidden = hidden + jnp.dot(
                    some, up[j * feat : (j + 1) * feat, :], preferred_element_type=F32
                )
            act[rows, :], slope[rows, :] = gelu(hidden)
            return 0

        lax.fori_loop(0, xn, rows_of, 0)

    steps = dict(
        x0=x0, x1=x1, x2=x2, x3=x3, p=project, k0=k0, k1=k1, k2=k2, k3=k3,
        qs=queries, ks=keys, g=greetings, prep=prepare, pred=predict,
    )
    for step in PLAN:
        steps[step[0]](*step[1:])

    def block_out(k):
        i = lax.rem(x + k, xn)
        for head, (_, total, acc) in enumerate(attend(i, N_X - 1)):
            feats_out[k, :, head] = (acc / total).astype(BF16).reshape(2, chunk, HD)
        if k == 0:
            copy = pltpu.make_async_copy(feats_out.at[k, zh], feats_in.at[tp], local.at[0])
            copy.start()
        else:
            to = along_x(k)
            send(("fa", k), feats_out.at[k, zh], feats_in.at[tp], fs.at[0, k], fr.at[0, k], at_tp(to))
            copy = None
        to = other(along_x(k))
        send(("fb", k), feats_out.at[k, 1 - zh], feats_in.at[tp], fs.at[1, k], fr.at[1, k], at_tp(to))
        return copy

    block_out(1)
    block_out(2)
    x2(STUDENT[1])
    block_out(3)
    block_out(0).wait()
    k3(PROBE)
    for k in range(xn):
        arrived(("fb", k))
        if k:
            arrived(("fa", k))
    grad_scale = 1.0 / math.sqrt(chunk * tps * toks * grps)

    def diff_of(i):
        target = jnp.zeros((chunk, feat), F32)
        for p in range(tps):
            feats = jnp.concatenate([feats_in[p, head] for head in range(heads)], axis=1)
            block = shared[:, p, i * piece_rows : (i + 1) * piece_rows, :].reshape(width, feat)
            target = target + jnp.dot(feats, block, preferred_element_type=F32)
        diff = out_pred[:, i * feat : (i + 1) * feat] - target
        xb[PRED[i] - 1, tp] = (diff * grad_scale).astype(BF16)
        x0(PRED[i])
        return diff

    diff_b = diff_of(1)
    diff_a = diff_of(0)
    squares = jnp.sum((diff_a * diff_a + diff_b * diff_b).reshape(chunk // 8, 8, feat), axis=0)
    loss_tp[tp] = sum(squares[:, i * 128 : (i + 1) * 128] for i in range(feat // 128))
    for d in range(1, tps):
        send(("lt", d), loss_tp.at[tp], loss_tp.at[tp], lt_s.at[d], lt_r.at[d], at_tp(tp_peer(d)))
    x3(STUDENT[0])
    x3(STUDENT[1])
    x1(PRED[1])
    x1(PRED[0])
    activate()
    x2(PRED[1])
    x2(PRED[0])
    x3(PRED[1])

    down_mine = down_raw[:, tp].reshape(act.shape[1], 2 * feat)

    def pred(c):
        return xb[c - 1].reshape(tps * chunk, feat)

    def grad_down_of(i):
        acc_down[:, :, :, i * feat : (i + 1) * feat] = lax.dot_general(
            act[...], pred(PRED[i]), (((0,), (0,)), ((), ())), preferred_element_type=F32
        ).reshape(gys, 2, -1, feat)

    def d_act_of(i):
        return lax.dot_general(
            pred(PRED[i]), down_mine[:, i * feat : (i + 1) * feat],
            (((1,), (1,)), ((), ())), preferred_element_type=F32,
        )

    d_act = d_act_of(1)
    grad_down_of(1)
    x3(PRED[0])
    d_hidden = ((d_act + d_act_of(0)) * slope[...]).astype(BF16)
    for i, c in enumerate(STUDENT):
        acc_up[i * gys // 2 : (i + 1) * gys // 2] = lax.dot_general(
            pred(c), d_hidden, (((0,), (0,)), ((), ())), preferred_element_type=F32,
        ).reshape(gys // 2, 2, -1, act.shape[1])
    send("cu", acc_up.at[:, 1 - core], core_up, co_s.at[2], co_r.at[2], to_sib)
    grad_down_of(0)
    send("cd", acc_down.at[:, 1 - core], core_down, co_s.at[0], co_r.at[0], to_sib)
    for d in range(1, tps):
        arrived(("lt", d))
    loss_core[core] = sum(loss_tp[i] for i in range(tps))
    send("cl", loss_core.at[core], loss_core.at[core], co_s.at[1], co_r.at[1], to_sib)

    arrived("cu")
    mine_up[...] = acc_up[:, core] + core_up[...]
    sent_up[...] = mine_up[...].astype(BF16)
    for d in range(1, gys):
        to = gy_peer(d)
        send(("gu", d), sent_up.at[to], got_up.at[d], gy_s.at[2, d], gy_r.at[2, d], at_gy(to))
    arrived("cd", "cl")
    mine_down[...] = acc_down[:, core] + core_down[...]
    sent_down[...] = mine_down[...].astype(BF16)
    loss_gy[gy] = loss_core[0] + loss_core[1]
    for d in range(1, gys):
        to = gy_peer(d)
        send(("gd", d), sent_down.at[to], got_down.at[d], gy_s.at[0, d], gy_r.at[0, d], at_gy(to))
        send(("gl", d), loss_gy.at[gy], loss_gy.at[gy], gy_s.at[1, d], gy_r.at[1, d], at_gy(to))
    total = mine_up[gy]
    for d in range(1, gys):
        arrived(("gu", d))
    for d in range(1, gys):
        total = total + got_up[d].astype(F32)
    up_rows[...] = total.reshape(up_rows.shape)
    for d in range(1, tps):
        q = tp_peer(d)
        send(("aa", d), up_rows.at[q], up_got.at[tp], aa_s.at[d], aa_r.at[d], at_tp(q))
    for d in range(1, gys):
        arrived(("gd", d), ("gl", d))
    total = mine_down[gy]
    for d in range(1, gys):
        total = total + got_down[d].astype(F32)
    down_out[...] = total
    loss[...] = sum(loss_gy[i] for i in range(gys))
    up_got[tp] = up_rows[tp]
    for d in range(1, tps):
        arrived(("aa", d))
    up_out[...] = up_got[...]
    for copy in sent.values():
        copy.wait_send()


def on_device(teacher_in, norm_gain, w_qkv, probe, student_in, w_up, w_down):
    grps, toks, tps = sizes = tuple(lax.axis_size(name) for name in ("grp", "tok", "tp"))
    gys, xn = grps * toks // 2, tps // 2
    rows, feat = teacher_in.shape
    depth, _, width = w_qkv.shape
    ff, ds = w_down.shape
    heads, units, chunk = width // HD, ff // tps, rows // N_X
    piece, strip = units // (2 * gys), ds // (2 * gys)
    gain = jnp.broadcast_to(norm_gain.astype(F32)[None, :], (8, feat))
    dma = pltpu.SemaphoreType.DMA
    vmem, hbm = pl.BlockSpec(memory_space=pltpu.VMEM), pl.BlockSpec(memory_space=pl.ANY)
    state = pltpu.VMEM((N_X // 2, heads, 2 * chunk, HD), F32)
    squares, grad_up, grad_down = pl.pallas_call(
        functools.partial(whole_kernel, sizes),
        name="distill",
        out_shape=(
            jax.ShapeDtypeStruct((8, 128), F32),
            jax.ShapeDtypeStruct((tps, strip // tps, units), F32),
            jax.ShapeDtypeStruct((piece, ds), F32),
        ),
        in_specs=[vmem, vmem, hbm, vmem, vmem, hbm, hbm],
        out_specs=[vmem] * 3,
        scratch_shapes=[
            pltpu.VMEM((len(FIRSTS) - 1, tps, chunk, feat), BF16),
            pltpu.VMEM((tps, 8, feat), F32),
            pltpu.VMEM((3, depth, width), BF16),
            pltpu.VMEM((chunk, depth), BF16),
            pltpu.VMEM((N_X, chunk, width), BF16),
            pltpu.VMEM((N_X, toks, chunk, 2 * width), BF16),
            state, state, state,
            pltpu.VMEM((ds, ff), BF16),
            pltpu.VMEM((ds, units), BF16),
            pltpu.VMEM((2 * gys, tps, piece, ds), BF16),
            pltpu.VMEM((rows, units), BF16),
            pltpu.VMEM((rows, units), F32),
            pltpu.VMEM((chunk, ds), F32),
            pltpu.VMEM((xn, 2, heads, chunk, HD), BF16),
            pltpu.VMEM((tps, heads, chunk, HD), BF16),
            pltpu.VMEM((toks, tps, 2 * width // toks, feat), BF16),
            pltpu.VMEM((gys, 2, piece, ds), F32),
            pltpu.VMEM((gys, 2, strip, units), F32),
            pltpu.VMEM((gys, piece, ds), F32),
            pltpu.VMEM((gys, strip, units), F32),
            pltpu.VMEM((gys, piece, ds), F32),
            pltpu.VMEM((gys, strip, units), F32),
            pltpu.VMEM((gys, piece, ds), BF16),
            pltpu.VMEM((gys, strip, units), BF16),
            pltpu.VMEM((gys, piece, ds), BF16),
            pltpu.VMEM((gys, strip, units), BF16),
            pltpu.VMEM((tps, strip // tps, units), F32),
            pltpu.VMEM((tps, strip // tps, units), F32),
            pltpu.VMEM((tps, 8, 128), F32),
            pltpu.VMEM((2, 8, 128), F32),
            pltpu.VMEM((gys, 8, 128), F32),
            dma((len(FIRSTS), len(NAMES_X))), dma((len(FIRSTS), len(NAMES_X))),
            dma((tps,)), dma((tps,)),
            dma((N_X + 1, len(NAMES_K))), dma((N_X + 1, len(NAMES_K))),
            dma((5 + N_X,)), dma((2, xn)), dma((2, xn)),
            dma((tps,)), dma((tps,)), dma((3,)), dma((3,)),
            dma((3, gys)), dma((3, gys)), dma((tps,)), dma((tps,)),
        ],
        compiler_params=pltpu.CompilerParams(
            collective_id=1, has_side_effects=True, vmem_limit_bytes=61 << 20
        ),
    )(
        teacher_in, gain, jnp.transpose(w_qkv, (1, 0, 2)), probe, student_in, w_up,
        w_down.reshape(2 * gys, tps, piece, ds),
    )
    grad_up = grad_up.reshape(tps, -1, 2 * gys, piece).transpose(1, 2, 0, 3).reshape(-1, ff)
    loss = jnp.sum(squares) / (chunk * tps * toks * grps * ds)
    return (loss, grad_up, grad_down)


def solution(mesh):
    placed = (
        P(("grp", "tok"), "tp"),
        P("tp"),
        P(None, None, "tp"),
        P("tp", None),
        P(("grp", "tok", "tp"), None),
        P(),
        P(),
    )
    return jax.shard_map(
        on_device,
        mesh=mesh,
        in_specs=placed,
        out_specs=(P(), P(("grp", "tok", "tp"), None), P(("grp", "tok", "tp"), None)),
        check_vma=False,
    )
```

```python
import functools
import math

import jax
import jax.numpy as jnp
from jax import lax
from jax.experimental import pallas as pl
from jax.experimental.pallas import tpu as pltpu
from jax.sharding import PartitionSpec as P

HD = 128
EXP2_SCALE = math.log2(math.e) / math.sqrt(HD)
MESH = pl.DeviceIdType.MESH
BF16, F32 = jnp.bfloat16, jnp.float32

FIRSTS = ("x", "z") * 7
N_X = 8
STUDENT = (N_X, N_X + 1)
PROBE = (N_X + 2, N_X + 3)
PRED = (N_X + 4, N_X + 5)
NAMES_X = ("z0", "z1", "z2", "z3", "r0", "l0", "r1", "l1", "fr0", "fr1", "fl0", "fl1")
NAMES_K = ("s0", "s1", "s2", "s3", "u0", "d0", "fu", "fd")


def make_plan(early=3):
    n, last = N_X, PROBE[1]
    plan = [("x0", 0), ("g",)] + [("x0", c) for c in range(1, early)]
    plan += [("prep",), ("x1", 0), ("x1", 1), ("x2", 0), ("pred",)]
    for c in range(n):
        plan += [("x0", c + early)] if c + early <= last else []
        plan += [("x1", c + 2), ("x2", c + 1)]
        if c >= 2:
            plan.append(("k2", c - 2))
        if c >= 3:
            plan.append(("k3", c - 3))
            if c % 2 == 0:
                plan.append(("ks", c // 2 - 1, 0, c - 3))
            plan.append(("qs", 0, c // 2, c - 3))
        if c >= 1:
            plan.append(("k1", c - 1))
        plan += [("x3", c), ("p", c)]
    plan += [("x0", c) for c in range(n + early, last + 1)]
    pair = n // 2 - 1
    plan += [
        ("k2", n - 2), ("ks", pair, 0, 2), ("x2", n + 1), ("x1", n + 2), ("ks", pair, 2, n - 3),
        ("k1", n - 1), ("x1", n + 3), ("x2", n + 2), ("k3", n - 3), ("qs", 0, n // 2, n - 3),
        ("k2", n - 1), ("x2", n + 3), ("x3", n), ("x3", n + 1), ("act",),
        ("k3", n - 2), ("x3", n + 2), ("x3", n + 3), ("share",), ("qs", 0, n // 2, n - 2),
        ("k3", n - 1),
    ]
    return tuple(plan)


PLAN = make_plan()


def whole_kernel(
    sizes, teacher_in, gain, w_hbm, probe, student, up_hbm, down_hbm,
    loss, up_out, down_out,
    xb, gains, w, normed, qb, kvb, top_s, sum_s, acc_s,
    up_raw, up, down_raw, act, slope, out_pred, feats_out, feats_in, probe_sib,
    acc_down, acc_up, core_down, core_up, mine_down, mine_up,
    sent_down, sent_up, got_down, got_up, up_rows, up_got,
    loss_tp, loss_core, loss_gy,
    xs, xr, gs, gr, ks, kr, local, fs, fr, ps, pr,
    lt_s, lt_r, co_s, co_r, gy_s, gy_r, aa_s, aa_r,
):
    grps, toks, tps = sizes
    xn, ys = tps // 2, toks // 2
    gys = grps * ys
    grp, tok, tp = lax.axis_index("grp"), lax.axis_index("tok"), lax.axis_index("tp")
    chunk, feat = xb.shape[2], xb.shape[3]
    half = chunk // 2
    width = qb.shape[2]
    heads = width // HD
    pair = 2 * chunk
    zh, x = lax.rem(tp, 2), tp // 2
    core, y = lax.rem(tok, 2), tok // 2
    gy = grp * ys + y
    zp = tp + 1 - 2 * zh

    def along_x(d):
        return lax.rem(x + d, xn) * 2 + zh

    def along_y(d):
        return lax.rem(y + d, ys) * 2 + core

    def other(slot):
        return slot + 1 - 2 * zh

    def tp_peer(d):
        return lax.rem(tp + d, tps)

    def gy_peer(d):
        return lax.rem(gy + d, gys)

    def at_tp(to):
        return (grp, tok, to)

    def at_gy(to):
        return (to // ys, lax.rem(to, ys) * 2 + core, tp)

    right, left, across = along_x(1), along_x(3), along_x(2)
    above, below, yfar = along_y(1), along_y(3), along_y(2)
    to_z, to_right, to_left = at_tp(zp), at_tp(right), at_tp(left)
    to_up, to_down = (grp, above, tp), (grp, below, tp)
    to_sib = (grp, tok + 1 - 2 * core, tp)

    def own_probe(i):
        return probe.at[pl.ds(pl.multiple_of(core * chunk, chunk), chunk), pl.ds(i * feat, feat)]

    fetch = [
        pltpu.make_async_copy(w_hbm, w, local.at[0]),
        pltpu.make_async_copy(up_hbm, up_raw, local.at[1]),
        pltpu.make_async_copy(down_hbm, down_raw, local.at[2]),
    ]
    keep = [
        pltpu.make_async_copy(
            teacher_in.at[pl.ds(c * chunk, chunk), :], xb.at[c, tp], local.at[3 + c]
        )
        for c in range(N_X)
    ] + [
        pltpu.make_async_copy(
            student.at[:, pl.ds(i * feat, feat)], xb.at[c, tp], local.at[3 + c]
        )
        for i, c in enumerate(STUDENT)
    ] + [
        pltpu.make_async_copy(own_probe(i), xb.at[c, tp], local.at[3 + c])
        for i, c in enumerate(PROBE)
    ]
    for copy in keep + fetch:
        copy.start()
    gains[tp] = gain[...]

    barrier = pltpu.get_barrier_semaphore()
    greet = [at_tp(tp_peer(d)) for d in range(1, tps)]
    greet += [at_gy(gy_peer(d)) for d in range(1, gys)] + [to_sib]
    for device in greet:
        pl.semaphore_signal(barrier, inc=1, device_id=device, device_id_type=MESH)
    pl.semaphore_wait(barrier, len(greet))

    sent = {}

    def send(name, src, dst, ssem, rsem, device):
        copy = pltpu.make_async_remote_copy(
            src_ref=src, dst_ref=dst, send_sem=ssem, recv_sem=rsem,
            device_id=device, device_id_type=MESH,
        )
        copy.start()
        sent[name] = copy

    def arrived(*names):
        for name in names:
            sent[name].wait_recv()


    def send_x(name, c, ref, device):
        i = NAMES_X.index(name)
        send((name, c), ref[0], ref[1], xs.at[c, i], xr.at[c, i], device)

    def own(c):
        to = xb.at[c, tp]
        if c < N_X:
            return teacher_in.at[pl.ds(c * chunk, chunk), :], to
        if c in STUDENT:
            return student.at[:, pl.ds((c - N_X) * feat, feat)], to
        if c in PROBE:
            return own_probe(c - PROBE[0]), to
        return to, to

    def slot(c, p):
        return xb.at[c, p], xb.at[c, p]

    def part(c, p, h):
        ref = xb.at[c, p, pl.ds(h * half, half), :]
        return ref, ref

    def x0(c):
        if FIRSTS[c] == "z":
            send_x("z0", c, own(c), to_z)
        send_x("r0", c, own(c), to_right)
        send_x("l0", c, own(c), to_left)
        if FIRSTS[c] == "x":
            send_x("z0", c, own(c), to_z)

    def x1(c):
        if FIRSTS[c] == "z":
            arrived(("z0", c))
            send_x("r1", c, slot(c, zp), to_right)
            send_x("l1", c, slot(c, zp), to_left)
        else:
            arrived(("r0", c))
            send_x("fr0", c, part(c, left, 0), to_right)
            send_x("z1", c, slot(c, left), to_z)
            arrived(("l0", c))
            send_x("fl0", c, part(c, right, 1), to_left)
            send_x("z2", c, slot(c, right), to_z)

    def x2(c):
        if FIRSTS[c] == "z":
            arrived(("r0", c))
            send_x("fr0", c, part(c, left, 0), to_right)
            arrived(("l0", c))
            send_x("fl0", c, part(c, right, 1), to_left)
            arrived(("r1", c))
            send_x("fr1", c, part(c, other(left), 0), to_right)
            arrived(("l1", c))
            send_x("fl1", c, part(c, other(right), 1), to_left)
        else:
            arrived(("fr0", c), ("fl0", c))
            send_x("z3", c, slot(c, across), to_z)

    def x3(c):
        if FIRSTS[c] == "z":
            arrived(("fr0", c), ("fl0", c), ("fr1", c), ("fl1", c))
        else:
            arrived(("z0", c), ("z1", c), ("z2", c), ("z3", c))

    def greetings():
        for d in range(1, tps):
            send(("g", d), gains.at[tp], gains.at[tp], gs.at[d], gr.at[d], at_tp(tp_peer(d)))
        top_s[...] = jnp.full(top_s.shape, -1e30, F32)
        sum_s[...] = jnp.zeros(sum_s.shape, F32)
        acc_s[...] = jnp.zeros(acc_s.shape, F32)

    def prepare():
        fetch[1].wait()
        ff, units = up_raw.shape[1], up.shape[1]
        piece = units // (2 * gys)
        step = 512

        def add(b, total):
            row = lax.broadcasted_iota(jnp.int32, (step, units), 0) + b * step
            col = lax.broadcasted_iota(jnp.int32, (step, units), 1)
            rest = jnp.bitwise_and(col, piece - 1)
            unit = (col - rest) * tps + tp * piece + rest
            pick = jnp.where(row == unit, 1.0, 0.0).astype(BF16)
            cols = pl.ds(pl.multiple_of(b * step, step), step)
            return total + jnp.dot(up_raw[:, cols], pick, preferred_element_type=F32)

        up[...] = lax.fori_loop(0, ff // step, add, jnp.zeros(up.shape, F32)).astype(BF16)
        fetch[0].wait()
        fetch[2].wait()
        for d in range(1, tps):
            arrived(("g", d))


    def send_k(name, c, ref, device):
        i = NAMES_K.index(name)
        send((name, c), ref, ref, ks.at[c, i], kr.at[c, i], device)

    def project(c):
        keep[c].wait()
        step = 64

        def rows_of(i, _):
            rows = pl.ds(pl.multiple_of(i * step, step), step)
            squares = jnp.zeros((step, feat), F32)
            for p in range(tps):
                some = xb[c, p, rows, :].astype(F32)
                squares = squares + some * some
            mean = jnp.sum(squares, axis=1, keepdims=True) / (tps * feat)
            scale = lax.rsqrt(mean + 1e-05)
            for p in range(tps):
                some = xb[c, p, rows, :].astype(F32)
                normed[rows, p * feat : (p + 1) * feat] = (
                    some * scale * gains[p, 0:1, :]
                ).astype(BF16)
            return 0

        lax.fori_loop(0, chunk // step, rows_of, 0)
        for j in (1, 2):
            kvb[c, tok, :, (j - 1) * width : j * width] = jnp.dot(
                normed[...], w[j], preferred_element_type=F32
            ).astype(BF16)
        send_k("u0", c, kvb.at[c, tok], to_up)
        send_k("d0", c, kvb.at[c, tok], to_down)
        send_k("s0", c, kvb.at[c, tok], to_sib)
        qb[c] = jnp.dot(normed[...], w[0], preferred_element_type=F32).astype(BF16)

    def k1(c):
        arrived(("u0", c))
        send_k("fu", c, kvb.at[c, below, pl.ds(0, half), :], to_up)
        send_k("s1", c, kvb.at[c, below], to_sib)
        arrived(("d0", c))
        send_k("fd", c, kvb.at[c, above, pl.ds(half, half), :], to_down)
        send_k("s2", c, kvb.at[c, above], to_sib)

    def k2(c):
        arrived(("fu", c), ("fd", c))
        send_k("s3", c, kvb.at[c, yfar], to_sib)

    def k3(c):
        arrived(("s0", c), ("s1", c), ("s2", c), ("s3", c))

    def attend(i, c):
        result = []
        for head in range(heads):
            cols = slice(head * HD, (head + 1) * HD)
            vcols = slice(width + head * HD, width + (head + 1) * HD)
            query = qb[pl.ds(2 * i, 2), :, cols].reshape(pair, HD)
            top = top_s[i, head][:, :1]
            keys = kvb[c, :, :, cols].reshape(toks * chunk, HD)
            values = kvb[c, :, :, vcols].reshape(toks * chunk, HD)
            scores = lax.dot_general(
                query, keys, (((1,), (1,)), ((), ())), preferred_element_type=F32
            )
            top_new = jnp.maximum(top, jnp.max(scores, axis=1, keepdims=True))
            fade = jnp.exp2((top - top_new) * EXP2_SCALE)
            weights = jnp.exp2(scores * EXP2_SCALE - top_new * EXP2_SCALE).astype(BF16)
            both = jnp.concatenate([values, jnp.ones_like(values)], axis=1)
            res = jnp.dot(weights, both, preferred_element_type=F32)
            result.append(
                (top_new, sum_s[i, head] * fade + res[:, HD:], acc_s[i, head] * fade + res[:, :HD])
            )
        return result

    def attend_keep(i, c):
        for head, (top, total, acc) in enumerate(attend(i, c)):
            top_s[i, head] = jnp.broadcast_to(top, (pair, HD))
            sum_s[i, head] = total
            acc_s[i, head] = acc
        return 0

    def queries(lo, hi, c):
        lax.fori_loop(lo, hi, lambda i, _: attend_keep(i, c), 0)

    def keys(i, lo, hi):
        lax.fori_loop(lo, hi, lambda c, _: attend_keep(i, c), 0)

    def gelu(hidden):
        rate = math.sqrt(2 / math.pi)
        square = hidden * hidden
        tanh = jnp.tanh(rate * (hidden + 0.044715 * (hidden * square)))
        cdf = 0.5 * (1.0 + tanh)
        rise = cdf + 0.5 * hidden * (1.0 - tanh * tanh) * (rate * (1.0 + 3 * 0.044715 * square))
        return (hidden * cdf).astype(BF16), rise

    def predict():
        step = 512
        out_pred[...] = jnp.zeros(out_pred.shape, F32)
        lead = step // (tps * down_raw.shape[2])

        def add(b, _):
            cols = pl.ds(pl.multiple_of(b * step, step), step)
            hidden = jnp.dot(student[...], up_raw[:, cols], preferred_element_type=F32)
            rows_down = down_raw[pl.ds(b * lead, lead)].reshape(step, down_raw.shape[3])
            out_pred[...] += jnp.dot(gelu(hidden)[0], rows_down, preferred_element_type=F32)
            return 0

        lax.fori_loop(0, up_raw.shape[1] // step, add, 0)

    def share():
        for i, c in enumerate(PROBE):
            keep[c].wait()
            send(("ps", i), xb.at[c], probe_sib.at[i], ps.at[i], pr.at[i], to_sib)

    def activate():
        for c in STUDENT:
            keep[c].wait()

        def rows_of(i, _):
            rows = pl.ds(pl.multiple_of(i * pair, pair), pair)
            hidden = jnp.zeros((pair, up.shape[1]), F32)
            for j, c in enumerate(STUDENT):
                some = xb[c, pl.ds(2 * i, 2)].reshape(pair, feat)
                hidden = hidden + jnp.dot(
                    some, up[j * feat : (j + 1) * feat, :], preferred_element_type=F32
                )
            act[rows, :], slope[rows, :] = gelu(hidden)
            return 0

        lax.fori_loop(0, xn, rows_of, 0)

    steps = dict(
        x0=x0, x1=x1, x2=x2, x3=x3, p=project, k1=k1, k2=k2, k3=k3,
        qs=queries, ks=keys, g=greetings, prep=prepare, act=activate, pred=predict, share=share,
    )
    for step in PLAN:
        steps[step[0]](*step[1:])

    def block_out(k):
        i = lax.rem(x + k, xn)
        for head, (_, total, acc) in enumerate(attend(i, N_X - 1)):
            feats_out[k, :, head] = (acc / total).astype(BF16).reshape(2, chunk, HD)
        if k == 0:
            copy = pltpu.make_async_copy(feats_out.at[k, zh], feats_in.at[tp], local.at[0])
            copy.start()
        else:
            to = along_x(k)
            send(("fa", k), feats_out.at[k, zh], feats_in.at[tp], fs.at[0, k], fr.at[0, k], at_tp(to))
            copy = None
        to = other(along_x(k))
        send(("fb", k), feats_out.at[k, 1 - zh], feats_in.at[tp], fs.at[1, k], fr.at[1, k], at_tp(to))
        return copy

    block_out(1)
    block_out(2)
    block_out(3)
    block_out(0).wait()
    arrived(("ps", 0), ("ps", 1))
    for k in range(xn):
        arrived(("fb", k))
        if k:
            arrived(("fa", k))
    mine = jnp.concatenate([feats_in[p, core] for p in range(tps)], axis=1)
    rest = jnp.concatenate([feats_in[p, 1 - core] for p in range(tps)], axis=1)
    grad_scale = 1.0 / math.sqrt(chunk * tps * toks * grps)

    def diff_of(i):
        target = jnp.dot(
            mine, xb[PROBE[i]].reshape(tps * chunk, feat), preferred_element_type=F32
        ) + jnp.dot(rest, probe_sib[i].reshape(tps * chunk, feat), preferred_element_type=F32)
        diff = out_pred[:, i * feat : (i + 1) * feat] - target
        xb[PRED[i], tp] = (diff * grad_scale).astype(BF16)
        x0(PRED[i])
        return diff

    diff_b = diff_of(1)
    diff_a = diff_of(0)
    squares = jnp.sum((diff_a * diff_a + diff_b * diff_b).reshape(chunk // 8, 8, feat), axis=0)
    loss_tp[tp] = sum(squares[:, i * 128 : (i + 1) * 128] for i in range(feat // 128))
    for d in range(1, tps):
        send(("lt", d), loss_tp.at[tp], loss_tp.at[tp], lt_s.at[d], lt_r.at[d], at_tp(tp_peer(d)))
    x1(PRED[1])
    x1(PRED[0])
    x2(PRED[1])
    x2(PRED[0])
    x3(PRED[1])

    down_mine = down_raw[:, tp].reshape(act.shape[1], 2 * feat)

    def pred(c):
        return xb[c].reshape(tps * chunk, feat)

    def grad_down_of(i):
        acc_down[:, :, :, i * feat : (i + 1) * feat] = lax.dot_general(
            act[...], pred(PRED[i]), (((0,), (0,)), ((), ())), preferred_element_type=F32
        ).reshape(gys, 2, -1, feat)

    def d_act_of(i):
        return lax.dot_general(
            pred(PRED[i]), down_mine[:, i * feat : (i + 1) * feat],
            (((1,), (1,)), ((), ())), preferred_element_type=F32,
        )

    grad_down_of(1)
    d_act = d_act_of(1)
    x3(PRED[0])
    grad_down_of(0)
    for d in range(1, tps):
        arrived(("lt", d))
    loss_core[core] = sum(loss_tp[i] for i in range(tps))
    send("cd", acc_down.at[:, 1 - core], core_down, co_s.at[0], co_r.at[0], to_sib)
    send("cl", loss_core.at[core], loss_core.at[core], co_s.at[1], co_r.at[1], to_sib)
    d_act = d_act + d_act_of(0)
    d_hidden = (d_act * slope[...]).astype(BF16)
    for i, c in enumerate(STUDENT):
        acc_up[i * gys // 2 : (i + 1) * gys // 2] = lax.dot_general(
            xb[c].reshape(tps * chunk, feat), d_hidden,
            (((0,), (0,)), ((), ())), preferred_element_type=F32,
        ).reshape(gys // 2, 2, -1, act.shape[1])
    send("cu", acc_up.at[:, 1 - core], core_up, co_s.at[2], co_r.at[2], to_sib)

    arrived("cd", "cl")
    mine_down[...] = acc_down[:, core] + core_down[...]
    sent_down[...] = mine_down[...].astype(BF16)
    loss_gy[gy] = loss_core[0] + loss_core[1]
    for d in range(1, gys):
        to = gy_peer(d)
        send(("gd", d), sent_down.at[to], got_down.at[d], gy_s.at[0, d], gy_r.at[0, d], at_gy(to))
        send(("gl", d), loss_gy.at[gy], loss_gy.at[gy], gy_s.at[1, d], gy_r.at[1, d], at_gy(to))
    arrived("cu")
    mine_up[...] = acc_up[:, core] + core_up[...]
    sent_up[...] = mine_up[...].astype(BF16)
    for d in range(1, gys):
        to = gy_peer(d)
        send(("gu", d), sent_up.at[to], got_up.at[d], gy_s.at[2, d], gy_r.at[2, d], at_gy(to))
    total = mine_up[gy]
    for d in range(1, gys):
        arrived(("gu", d))
    for d in range(1, gys):
        total = total + got_up[d].astype(F32)
    up_rows[...] = total.reshape(up_rows.shape)
    for d in range(1, tps):
        q = tp_peer(d)
        send(("aa", d), up_rows.at[q], up_got.at[tp], aa_s.at[d], aa_r.at[d], at_tp(q))
    for d in range(1, gys):
        arrived(("gd", d), ("gl", d))
    total = mine_down[gy]
    for d in range(1, gys):
        total = total + got_down[d].astype(F32)
    down_out[...] = total
    loss[...] = sum(loss_gy[i] for i in range(gys))
    up_got[tp] = up_rows[tp]
    for d in range(1, tps):
        arrived(("aa", d))
    up_out[...] = up_got[...]
    for copy in sent.values():
        copy.wait_send()


def on_device(teacher_in, norm_gain, w_qkv, probe, student_in, w_up, w_down):
    grps, toks, tps = sizes = tuple(lax.axis_size(name) for name in ("grp", "tok", "tp"))
    gys, xn = grps * toks // 2, tps // 2
    rows, feat = teacher_in.shape
    depth, _, width = w_qkv.shape
    ff, ds = w_down.shape
    heads, units, chunk = width // HD, ff // tps, rows // N_X
    piece, strip = units // (2 * gys), ds // (2 * gys)
    gain = jnp.broadcast_to(norm_gain.astype(F32)[None, :], (8, feat))
    dma = pltpu.SemaphoreType.DMA
    vmem, hbm = pl.BlockSpec(memory_space=pltpu.VMEM), pl.BlockSpec(memory_space=pl.ANY)
    state = pltpu.VMEM((N_X // 2, heads, 2 * chunk, HD), F32)
    squares, grad_up, grad_down = pl.pallas_call(
        functools.partial(whole_kernel, sizes),
        name="distill",
        out_shape=(
            jax.ShapeDtypeStruct((8, 128), F32),
            jax.ShapeDtypeStruct((tps, strip // tps, units), F32),
            jax.ShapeDtypeStruct((piece, ds), F32),
        ),
        in_specs=[vmem, vmem, hbm, vmem, vmem, hbm, hbm],
        out_specs=[vmem] * 3,
        scratch_shapes=[
            pltpu.VMEM((len(FIRSTS), tps, chunk, feat), BF16),
            pltpu.VMEM((tps, 8, feat), F32),
            pltpu.VMEM((3, depth, width), BF16),
            pltpu.VMEM((chunk, depth), BF16),
            pltpu.VMEM((N_X, chunk, width), BF16),
            pltpu.VMEM((N_X, toks, chunk, 2 * width), BF16),
            state, state, state,
            pltpu.VMEM((ds, ff), BF16),
            pltpu.VMEM((ds, units), BF16),
            pltpu.VMEM((2 * gys, tps, piece, ds), BF16),
            pltpu.VMEM((rows, units), BF16),
            pltpu.VMEM((rows, units), F32),
            pltpu.VMEM((chunk, ds), F32),
            pltpu.VMEM((xn, 2, heads, chunk, HD), BF16),
            pltpu.VMEM((tps, heads, chunk, HD), BF16),
            pltpu.VMEM((2, tps, chunk, feat), BF16),
            pltpu.VMEM((gys, 2, piece, ds), F32),
            pltpu.VMEM((gys, 2, strip, units), F32),
            pltpu.VMEM((gys, piece, ds), F32),
            pltpu.VMEM((gys, strip, units), F32),
            pltpu.VMEM((gys, piece, ds), F32),
            pltpu.VMEM((gys, strip, units), F32),
            pltpu.VMEM((gys, piece, ds), BF16),
            pltpu.VMEM((gys, strip, units), BF16),
            pltpu.VMEM((gys, piece, ds), BF16),
            pltpu.VMEM((gys, strip, units), BF16),
            pltpu.VMEM((tps, strip // tps, units), F32),
            pltpu.VMEM((tps, strip // tps, units), F32),
            pltpu.VMEM((tps, 8, 128), F32),
            pltpu.VMEM((2, 8, 128), F32),
            pltpu.VMEM((gys, 8, 128), F32),
            dma((len(FIRSTS), len(NAMES_X))), dma((len(FIRSTS), len(NAMES_X))),
            dma((tps,)), dma((tps,)),
            dma((N_X, len(NAMES_K))), dma((N_X, len(NAMES_K))),
            dma((3 + PRED[0],)), dma((2, xn)), dma((2, xn)), dma((2,)), dma((2,)),
            dma((tps,)), dma((tps,)), dma((3,)), dma((3,)),
            dma((3, gys)), dma((3, gys)), dma((tps,)), dma((tps,)),
        ],
        compiler_params=pltpu.CompilerParams(
            collective_id=1, has_side_effects=True, vmem_limit_bytes=61 << 20
        ),
    )(
        teacher_in, gain, jnp.transpose(w_qkv, (1, 0, 2)), probe, student_in, w_up,
        w_down.reshape(2 * gys, tps, piece, ds),
    )
    grad_up = grad_up.reshape(tps, -1, 2 * gys, piece).transpose(1, 2, 0, 3).reshape(-1, ff)
    loss = jnp.sum(squares) / (chunk * tps * toks * grps * ds)
    return (loss, grad_up, grad_down)


def solution(mesh):
    placed = (
        P(("grp", "tok"), "tp"),
        P("tp"),
        P(None, None, "tp"),
        P("tp", None),
        P(("grp", "tok", "tp"), None),
        P(),
        P(),
    )
    return jax.shard_map(
        on_device,
        mesh=mesh,
        in_specs=placed,
        out_specs=(P(), P(("grp", "tok", "tp"), None), P(("grp", "tok", "tp"), None)),
        check_vma=False,
    )
```
